256 devices in a mesh: ctx: 16 (over x, z_lo), head: 16 (over y, z_hi, core).
Axes of the slice: x: 4, y: 4, z: 8 (z_hi: 2, z_lo: 4; z = z_hi * 4 + z_lo), core: 2. Of those that a mesh axis runs over, the one named last changes fastest.
Arguments:
- hidden: bfloat16 [2048, 6144], P('ctx', 'head'), may hold values from -6 to 6
- fresh: bfloat16 [128, 6144], replicated, may hold values from -6 to 6
- w_qkv: bfloat16 [3, 6144, 6144], P(None, 'ctx', 'head'), may hold values from -0.076546554 to 0.076546554
- w_out: bfloat16 [6144, 6144], P('head', 'ctx'), may hold values from -0.109375 to 0.109375
- mod_table: float32 [3, 8, 6144], replicated, may hold values from -17 to 17
- levels: int32 [2, 16], replicated, may hold values from 0 to 7
- block_mask: int32 [16, 16], replicated, may hold values from 0 to 1, as said below
- counts: int32 [17], replicated, may hold values from 1 to 128, as said below
Outputs:
- denoised: bfloat16 [2048, 6144], P('ctx', 'head')
The draws below stay inside these ranges and needn't reach their ends.
Inputs may be any that keep to these rules, and one draw needn't show every extreme that they name: `block_mask`: entry [i, j] is 1 for j = i, 0 for j > i, and 1 or 0 for j < i. `counts`: entry p + s holds the valid tokens of window position p at step s; entry 16 belongs to the entering block; some entry equals 128.
All inputs are finite; a program needn't handle non-finite values. Where the reference program divides by a largest or mean magnitude, that divisor is 1e-20 or more.
Results may differ from the reference program's by a relative error of at most 0.035.
Values may be sent and summed in bfloat16 or wider, within the bound.
No kernel may reach another device: no remote copies, remote signals or barrier semaphores. Data moves between devices by JAX's collectives and lax.ppermute only.
A program may use at most 128 MiB of HBM per device.

```python
import jax
import jax.numpy as jnp
from jax import lax

D = 6144
HD = 128
TOK_DEV = 128
LEVELS = 8
STEPS = 2
BLOCKS = 16
TOKENS = 2048
N_HEAD = 16


def draw_block_mask(key, part):
    key = jax.random.fold_in(key, 11)
    rows = jnp.arange(BLOCKS, dtype=jnp.int32)[:, None]
    cols = jnp.arange(BLOCKS, dtype=jnp.int32)[None, :]
    coin = jax.random.randint(key, (BLOCKS, BLOCKS), 0, 4)
    earlier = (cols < rows) & (coin > 0)
    return jnp.where(cols == rows, 1, jnp.where(earlier, 1, 0)).astype(jnp.int32)


def draw_counts(key, part):
    key = jax.random.fold_in(key, 23)
    first_key, second_key = jax.random.split(key)
    lowest = max(1, TOK_DEV // 4)
    values = jax.random.randint(first_key, (BLOCKS + 1,), lowest, TOK_DEV + 1)
    fullest = jax.random.randint(second_key, (), 0, BLOCKS + 1)
    places = jnp.arange(BLOCKS + 1, dtype=jnp.int32)
    return jnp.where(places == fullest, TOK_DEV, values).astype(jnp.int32)


def draw_w_qkv(key, part):
    key = jax.random.fold_in(key, 31)
    bound = 6.0 * D ** (-0.5)
    base = jax.random.normal(key, (3, D, D), jnp.float32) * D ** (-0.5)
    return jnp.clip(base, -bound, bound).astype(jnp.bfloat16)


def draw_mod_table(key, part):
    key = jax.random.fold_in(key, 37)
    base = jnp.clip(jax.random.normal(key, (3, LEVELS, D), jnp.float32) * 0.5, -3.0, 3.0)
    return base.astype(jnp.float32)


def with_ends(drawn, own_key, least, top_value):
    index_at = [jax.random.randint(jax.random.fold_in(own_key, axis), (), 0, length) for axis, length in enumerate(drawn.shape)]
    main_axis = drawn.shape.index(max(drawn.shape))
    neighbour = index_at[:main_axis] + [(index_at[main_axis] + 1) % drawn.shape[main_axis]] + index_at[main_axis + 1:]
    return drawn.at[tuple(index_at)].set(least).at[tuple(neighbour)].set(top_value)


def spiked(drawn, rng, source, target, blocks, factor):
    owner, partner = [(jnp.arange(drawn.shape[dim]) // (drawn.shape[dim] // blocks)).reshape([-1 if axis == dim else 1 for axis in range(drawn.ndim)]) for dim in (source, target)]
    chosen = jax.random.permutation(rng, blocks)[partner]
    strong = (owner == chosen) | (owner == (partner + blocks // 2) % blocks)
    return jnp.where(strong, factor * drawn, drawn)


def block_levels(rng, extent, shards, smallest, high):
    level = 1.0
    for dim, blocks in shards:
        draws = jax.random.uniform(jax.random.fold_in(jax.random.fold_in(rng, 6), dim), (blocks,), jnp.float32, smallest / len(shards), high / len(shards))
        level = level * jnp.repeat(jnp.exp(draws), extent[dim] // blocks).reshape((-1,) + (1,) * (len(extent) - 1 - dim))
    return level


def centred(own_key, extent, width, most, cuts=(), kind=jnp.bfloat16):
    result = jax.random.normal(own_key, extent, jnp.float32) * width
    if len(cuts) > 0:
        result = block_levels(own_key, extent, cuts, -0.22, 0.18) * result
    return jnp.clip(result, min=-most, max=most).astype(kind)


def noise_with(stream_key, dims, scale, limit, pieces, heavy, held_as=jnp.bfloat16):
    result = scale * jax.random.normal(stream_key, dims, jnp.float32)
    if pieces:
        result = result * block_levels(stream_key, dims, pieces, -0.22, 0.18)
    return jnp.clip(spiked(result, jax.random.fold_in(stream_key, 3), *heavy), -limit, limit).astype(held_as)


def setup_inputs(seed: int = 0) -> dict:
    splits = jax.random.split(jax.random.key(seed), 9)
    hidden = centred(splits[0], (TOKENS, D), 1.0, 6.0, ((0, 16), (1, 16)))
    fresh = centred(splits[1], (TOK_DEV, D), 1.0, 6.0)
    w_qkv = draw_w_qkv(jax.random.fold_in(splits[8], 71), 0)
    w_out = noise_with(splits[3], (D, D), D ** -0.5, 0.109375, ((0, 16), (1, 16)), (0, 1, 16, 2.0))
    mod_table = draw_mod_table(jax.random.fold_in(splits[8], 71), 0)
    levels = with_ends(jax.random.randint(splits[5], (STEPS, BLOCKS), 0, LEVELS), jax.random.fold_in(splits[5], 1), 0, LEVELS - 1).astype(jnp.int32)
    block_mask = draw_block_mask(jax.random.fold_in(splits[8], 71), 0)
    counts = draw_counts(jax.random.fold_in(splits[8], 71), 0)
    return dict(hidden=hidden, fresh=fresh, w_qkv=w_qkv, w_out=w_out, mod_table=mod_table, levels=levels, block_mask=block_mask, counts=counts)


KEY_BOUND = 8.0
NEG = -1e+30

def layer(x, lev, cnt, w_qkv, w_out, mod_table, block_mask):
    onehot = (lev[:, None] == jnp.arange(LEVELS, dtype=jnp.int32)[None, :]).astype(jnp.float32)
    mods = jnp.einsum('cl,kld->kcd', onehot, mod_table, precision=lax.Precision.HIGHEST)
    mods = jnp.repeat(mods, TOK_DEV, axis=1)
    xf = x.astype(jnp.float32)
    normed = xf * lax.rsqrt(lax.optimization_barrier(jnp.mean(xf * xf, axis=-1, keepdims=True)) + 1e-06)
    h = (normed * (1.0 + mods[1]) + mods[0]).astype(jnp.bfloat16)
    query = jnp.dot(h, w_qkv[0], preferred_element_type=jnp.float32)
    keys = jnp.dot(h, w_qkv[1], preferred_element_type=jnp.float32)
    values = jnp.dot(h, w_qkv[2], preferred_element_type=jnp.float32)
    heads = D // HD
    keys3 = keys.reshape(TOKENS, heads, HD)
    amax = lax.optimization_barrier(jnp.max(jnp.abs(keys3), axis=(0, 1)))
    factor = KEY_BOUND / (amax + 1e-06) * HD ** (-0.5)
    q_hat = (query.reshape(TOKENS, heads, HD) * factor).astype(jnp.bfloat16)
    k_c = keys3.astype(jnp.bfloat16)
    v_c = values.reshape(TOKENS, heads, HD).astype(jnp.bfloat16)
    pos = jnp.arange(TOKENS, dtype=jnp.int32)
    block = pos // TOK_DEV
    inner = pos % TOK_DEV
    allowed = (block_mask[block][:, block] == 1) & (inner < cnt[block])[None, :]

    def one_head(args):
        qh, kh, vh = args
        scores = jnp.dot(qh, kh.T, preferred_element_type=jnp.float32)
        scores = jnp.where(allowed, scores, NEG)
        top = lax.optimization_barrier(jnp.max(scores, axis=-1, keepdims=True))
        weights = jnp.where(allowed, jnp.exp(scores - top), 0.0)
        denom = lax.optimization_barrier(jnp.sum(weights, axis=-1, keepdims=True))
        out = jnp.dot(weights.astype(jnp.bfloat16), vh, preferred_element_type=jnp.float32) / denom
        return out.astype(jnp.bfloat16)
    attended = lax.map(one_head, (q_hat.transpose(1, 0, 2), k_c.transpose(1, 0, 2), v_c.transpose(1, 0, 2)))
    attended = attended.transpose(1, 0, 2).reshape(TOKENS, D)
    group = D // N_HEAD

    def add_group(total, index):
        start = index * group
        part = jnp.dot(lax.dynamic_slice_in_dim(attended, start, group, 1), lax.dynamic_slice_in_dim(w_out, start, group, 0), preferred_element_type=jnp.float32)
        rounded = lax.optimization_barrier(part.astype(jnp.bfloat16))
        return (total + rounded.astype(jnp.float32), None)
    summed, _ = lax.scan(add_group, jnp.zeros((TOKENS, D), jnp.float32), jnp.arange(N_HEAD, dtype=jnp.int32))
    return (xf + mods[2] * summed).astype(jnp.bfloat16)

def reference(hidden, fresh, w_qkv, w_out, mod_table, levels, block_mask, counts):
    first = layer(hidden, levels[0], counts[0:BLOCKS], w_qkv, w_out, mod_table, block_mask)
    second_in = jnp.concatenate([first[TOK_DEV:], fresh], axis=0)
    return layer(second_in, levels[1], counts[1:BLOCKS + 1], w_qkv, w_out, mod_table, block_mask)
```

```python
import jax
import jax.numpy as jnp
from jax import lax
from jax.experimental import pallas as pl
from jax.experimental.pallas import tpu as pltpu
from jax.sharding import PartitionSpec as P

HD = 128
TOK = 128
W = 384
BLOCKS = 16
KEY_BOUND = 8.0
NEG = -1e30
F32 = jnp.float32
BF16 = jnp.bfloat16

BOTH = ("ctx", "head")


def coords():
    return [(x, zl, y, zh, core) for x in range(4) for zl in range(4) for y in range(4) for zh in range(2) for core in range(2)]


def flat(x, zl, y, zh, core):
    return ((x * 4 + zl) * 4 + y) * 4 + zh * 2 + core


def x_shift(a, t):
    return lax.ppermute(a, "ctx", [(c, (c + 4 * t) % 16) for c in range(16)])


def zl_shift(a, t):
    return lax.ppermute(a, "ctx", [(c, c // 4 * 4 + (c + t) % 4) for c in range(16)])


def y_shift(a, t):
    return lax.ppermute(a, "head", [(g, (g + 4 * t) % 16) for g in range(16)])


def quad_shift(a, t):
    return lax.ppermute(a, "head", [(g, g // 4 * 4 + (g + t) % 4) for g in range(16)])


def core_swap(a):
    return lax.ppermute(a, "head", [(g, g ^ 1) for g in range(16)])


def turned(a, flip):
    pairs = [(flat(x, zl, y, zh, core), flat(y, zl, x, zh ^ flip, core)) for x, zl, y, zh, core in coords()]
    return lax.ppermute(a, BOTH, pairs)


def block_back(a, flip):
    pairs = []
    for x, zl, y, zh, core in coords():
        to_y, to_zl = divmod((y * 4 + zl + 15) % 16, 4)
        pairs.append((flat(x, zl, y, zh, core), flat(x, to_zl, to_y, zh ^ flip, core)))
    return lax.ppermute(a, BOTH, pairs)


def call(kernel, outs, scratch=(), smem=0, n_in=0):
    specs = [pl.BlockSpec(memory_space=pltpu.SMEM)] * smem + [pl.BlockSpec(memory_space=pltpu.VMEM)] * n_in
    return pl.pallas_call(
        kernel,
        out_shape=[jax.ShapeDtypeStruct(s, d) for s, d in outs],
        in_specs=specs,
        out_specs=[pl.BlockSpec(memory_space=pltpu.VMEM)] * len(outs),
        scratch_shapes=list(scratch),
        compiler_params=pltpu.CompilerParams(vmem_limit_bytes=40 * 1024 * 1024),
    )


def square_kernel(*refs):
    own, other, out = refs[0:4], refs[4:8], refs[8]
    column = lax.broadcasted_iota(jnp.int32, (TOK, 128), 1)
    table = jnp.zeros((TOK, 128), F32)
    for s in range(4):
        a = own[s][...].astype(F32)
        b = other[s][...].astype(F32)
        total = jnp.sum(a * a + b * b, axis=1, keepdims=True)
        table = jnp.where(column == s, total, table)
    out[...] = table.T[0:8, :]


def squares(own, other):
    return call(square_kernel, [((8, 128), F32)], n_in=8)(*own, *other)[0]


def dot(a, b):
    return jnp.dot(a, b, preferred_element_type=F32)


def key_kernel(place, *refs):
    own, other, sums, mods, weights = refs[0:4], refs[4:8], refs[8:12], refs[12:16], refs[16:20]
    h_ref, own_out, sends = refs[20], refs[21], refs[22:25]
    turn, zl, core = place[0], place[1], place[2]
    total = sums[0][...] + sums[1][...] + sums[2][...] + sums[3][...]
    r = lax.rsqrt(total * (1.0 / (16 * W)) + 1e-06)
    r_t = jnp.concatenate([r] * 16, axis=0).T
    for s in range(4):
        t = (turn - s) & 3
        rows = pl.ds(pl.multiple_of(t * TOK, TOK), TOK)
        for tiles, scale, shift, c in (
            (own, mods[0], mods[1], core),
            (other, mods[2], mods[3], 1 - core),
        ):
            normed = tiles[s][...].astype(F32) * r_t[:, s : s + 1]
            h = (normed * (1.0 + scale[s : s + 1, :]) + shift[s : s + 1, :]).astype(BF16)
            for half in range(2):
                ring = (zl - (2 * half + c)) & 3
                h_ref[ring, rows, :] = h[:, half * W : (half + 1) * W]
    acc = dot(h_ref[0], weights[0][...])
    for ring in range(1, 4):
        acc = acc + dot(h_ref[ring], weights[ring][...])
    own_out[...] = acc[0:TOK]
    for t in range(1, 4):
        sends[t - 1][...] = acc[t * TOK : (t + 1) * TOK].astype(BF16)


def value_query_kernel(h_ref, *refs):
    weights, own_out, sends = (refs[0:4], refs[4:8]), refs[8], refs[9:12]
    for part in range(2):
        cols = slice(part * W, (part + 1) * W)
        acc = dot(h_ref[0], weights[part][0][...])
        for ring in range(1, 4):
            acc = acc + dot(h_ref[ring], weights[part][ring][...])
        own_out[:, cols] = acc[0:TOK]
        for t in range(1, 4):
            sends[t - 1][:, cols] = acc[t * TOK : (t + 1) * TOK].astype(BF16)


def key_sum_kernel(own, a, b, c, key_out, top_out):
    k = own[...] + a[...].astype(F32) + b[...].astype(F32) + c[...].astype(F32)
    key_out[...] = k.astype(BF16)
    k = jnp.abs(k)
    k = jnp.maximum(jnp.maximum(k[:, 0:HD], k[:, HD : 2 * HD]), k[:, 2 * HD :])
    top_out[...] = jnp.broadcast_to(jnp.max(k, axis=0, keepdims=True), (8, HD))


def value_query_sum_kernel(own, a, b, c, value_out, query_out):
    v = own[...] + a[...].astype(F32) + b[...].astype(F32) + c[...].astype(F32)
    value_out[...] = v[:, 0:W].astype(BF16)
    query_out[...] = v[:, W:].astype(BF16)


def attend_kernel(limits, *refs):
    queries, keys, values, amax, outs = refs[0:4], refs[4:8], refs[8:12], refs[12], refs[13:17]
    factor = KEY_BOUND / (amax[0:1, :] + 1e-06) * HD ** (-0.5)
    column = lax.broadcasted_iota(jnp.int32, (1, 4 * TOK), 1)
    inner = column % TOK
    col128 = lax.broadcasted_iota(jnp.int32, (TOK, 128), 1)
    for t in range(4):
        limit = jnp.zeros((1, 4 * TOK), jnp.int32)
        for u in range(4):
            limit = jnp.where(column // TOK == u, limits[t * 4 + u], limit)
        allowed = jnp.broadcast_to(inner < limit, (TOK, 4 * TOK))
        stats = jnp.zeros((TOK, 128), F32)
        for head in range(3):
            cols = slice(head * HD, (head + 1) * HD)
            q = (queries[t][:, cols].astype(F32) * factor).astype(BF16)
            k = jnp.concatenate([ref[:, cols] for ref in keys], axis=0)
            v = jnp.concatenate([ref[:, cols] for ref in values], axis=0)
            s = lax.dot_general(q, k, (((1,), (1,)), ((), ())), preferred_element_type=F32)
            s = jnp.where(allowed, s, NEG)
            top = jnp.max(s, axis=1, keepdims=True)
            w = jnp.where(allowed, jnp.exp(s - top), 0.0)
            total = jnp.sum(w, axis=1, keepdims=True)
            some = total > 0.0
            safe = jnp.where(some, total, 1.0)
            outs[t][:, cols] = (dot(w.astype(BF16), v) / safe).astype(BF16)
            lse = jnp.where(some, top + jnp.log(safe), NEG)
            for piece in range(3):
                part = lse.astype(BF16).astype(F32)
                stats = jnp.where(col128 == head * 3 + piece, part, stats)
                lse = lse - part
        outs[t][:, W:] = stats.astype(BF16)


def merge_kernel(*refs):
    parts, out = refs[0:4], refs[4]
    stats = [p[:, W:].astype(F32) for p in parts]
    for head in range(3):
        cols = slice(head * HD, (head + 1) * HD)
        at = head * 3
        lse = [s[:, at : at + 1] + s[:, at + 1 : at + 2] + s[:, at + 2 : at + 3] for s in stats]
        top = jnp.maximum(jnp.maximum(lse[0], lse[1]), jnp.maximum(lse[2], lse[3]))
        share = [jnp.exp(e - top) for e in lse]
        acc = share[0] * parts[0][:, cols].astype(F32)
        for i in range(1, 4):
            acc = acc + share[i] * parts[i][:, cols].astype(F32)
        out[:, cols] = (acc / (share[0] + share[1] + share[2] + share[3])).astype(BF16)


def project_kernel(place, *refs):
    attended, weights, out, o_all, w_all = refs[0:4], refs[4:8], refs[8], refs[9], refs[10]
    turn, zl, parity = place[0], place[1], place[2]
    for t in range(4):
        o_all[t] = attended[t][...]
        w_all[t] = weights[t][...]
    rows = jnp.concatenate([o_all[(turn + s) & 3] for s in range(4)], axis=0)
    for half in range(2):
        ring = (zl - (2 * half + parity)) & 3
        out[:, half * W : (half + 1) * W] = dot(rows, w_all[ring]).astype(BF16)


def project(place, attended, weights):
    return call(
        project_kernel,
        [((4 * TOK, 2 * W), BF16)],
        scratch=[pltpu.VMEM((4, TOK, W), BF16), pltpu.VMEM((4, W, W), BF16)],
        smem=1,
        n_in=8,
    )(place, *attended, *weights)[0]


def core_sum_kernel(a, b, own, *sends):
    own[...] = a[0:TOK].astype(F32) + b[0:TOK].astype(F32)
    for s in range(1, 4):
        rows = slice(s * TOK, (s + 1) * TOK)
        sends[s - 1][...] = (a[rows].astype(F32) + b[rows].astype(F32)).astype(BF16)


def y_sum_kernel(own, a, b, c, out):
    out[...] = (own[...] + a[...].astype(F32) + b[...].astype(F32) + c[...].astype(F32)).astype(BF16)


def pick(flag, a, b):
    return jnp.where(flag, a, b)


def on_device(hidden, fresh, w_qkv, w_out, mod_table, levels, block_mask, counts):
    ctx_at = lax.axis_index("ctx")
    head_at = lax.axis_index("head")
    x, zl = ctx_at // 4, ctx_at % 4
    y, zh, core = head_at // 4, (head_at // 2) % 2, head_at % 2
    four = jnp.arange(4, dtype=jnp.int32)
    ids = jnp.arange(BLOCKS, dtype=jnp.int32)

    a0, a1 = turned(hidden, 0), turned(hidden, 1)
    pair = pick(zh == 0, jnp.concatenate([a0, a1], 1), jnp.concatenate([a1, a0], 1))

    def ring(a):
        out = [a]
        for _ in range(3):
            out.append(zl_shift(out[-1], 1))
        return out

    wk, wv, wq, wo = ring(w_qkv[1]), ring(w_qkv[2]), ring(w_qkv[0]), ring(w_out)

    mine = lax.dynamic_slice_in_dim(mod_table, x * 4 * W, 4 * W, 2).reshape(3, -1, 2, 2, W)
    by_core = [mine[:, :, :, c].reshape(3, -1, 2 * W) for c in range(2)]
    mod_own = pick(core == 0, by_core[0], by_core[1])
    mod_other = pick(core == 0, by_core[1], by_core[0])
    level_ids = jnp.arange(mod_table.shape[1], dtype=jnp.int32)

    def rows_at(table, level):
        hot = level[..., None] == level_ids
        return jnp.sum(jnp.where(hot[..., None], table, 0.0), axis=-2)

    def level_of(step, blocks):
        return jnp.sum(jnp.where(blocks[..., None] == ids, levels[step], 0), axis=-1)

    slot_blocks = (y - four) % 4 * 4 + zl
    dest_block = y * 4 + zl
    gate_first = rows_at(mod_own[2], level_of(0, dest_block + 1))
    own_cols = lax.dynamic_slice_in_dim(mod_table[2], head_at * W, W, 1)
    gate_second = rows_at(own_cols, level_of(1, ctx_at))
    fresh_mine = lax.dynamic_slice_in_dim(fresh, x * 4 * W, 4 * W, 1).reshape(TOK, 2, 2, W)
    fresh_pair = pick(core == 0, fresh_mine[:, :, 0], fresh_mine[:, :, 1]).reshape(TOK, 2 * W)

    key_place = jnp.stack([(y - x) % 4, zl, core]).astype(jnp.int32)
    keep_place = jnp.stack([(x - y) % 4, zl, core]).astype(jnp.int32)
    send_place = jnp.stack([(x - y) % 4, zl, 1 - core]).astype(jnp.int32)
    query_blocks = (x - four) % 4 * 4 + zl
    key_blocks = x * 4 + (zl - four) % 4
    seen = jnp.sum(jnp.where((query_blocks[:, None] == ids)[..., None], block_mask, 0), axis=1)
    seen = jnp.sum(jnp.where(key_blocks[:, None] == ids, seen[:, None, :], 0), axis=-1)

    def layer(pair, step):
        lv = level_of(step, slot_blocks)
        mods = [rows_at(mod_own[1], lv), rows_at(mod_own[0], lv), rows_at(mod_other[1], lv), rows_at(mod_other[0], lv)]
        live = jnp.sum(jnp.where(key_blocks[:, None] == ids, counts[step : step + BLOCKS], 0), axis=-1)
        limits = (seen * live).reshape(16).astype(jnp.int32)

        own = [pair] + [y_shift(pair, s) for s in (1, 2, 3)]
        other = [core_swap(a) for a in own]
        sq = squares(own, other)
        sums = [sq] + [x_shift(sq, t) for t in (1, 2, 3)]
        h, k_own, *k_sends = call(
            key_kernel,
            [((4, 4 * TOK, W), BF16), ((TOK, W), F32)] + [((TOK, W), BF16)] * 3,
            smem=1,
            n_in=20,
        )(key_place, *own, *other, *sums, *mods, *wk)
        k_got = [x_shift(k_sends[t - 1], t) for t in (1, 2, 3)]
        vq_own, *vq_sends = call(
            value_query_kernel,
            [((TOK, 2 * W), F32)] + [((TOK, 2 * W), BF16)] * 3,
            n_in=9,
        )(h, *wv, *wq)
        vq_got = [x_shift(vq_sends[t - 1], t) for t in (1, 2, 3)]
        k_c, amax = call(key_sum_kernel, [((TOK, W), BF16), ((8, HD), F32)], n_in=4)(k_own, *k_got)
        for shift in (x_shift, y_shift, zl_shift, quad_shift):
            got = [shift(amax, t) for t in (1, 2, 3)]
            amax = jnp.maximum(jnp.maximum(amax, got[0]), jnp.maximum(got[1], got[2]))
        keys = [k_c] + [zl_shift(k_c, u) for u in (1, 2, 3)]
        v_c, q_b = call(value_query_sum_kernel, [((TOK, W), BF16)] * 2, n_in=4)(vq_own, *vq_got)
        values = [v_c] + [zl_shift(v_c, u) for u in (1, 2, 3)]
        queries = [q_b] + [x_shift(q_b, t) for t in (1, 2, 3)]
        parts = call(attend_kernel, [((TOK, W + 128), BF16)] * 4, smem=1, n_in=13)(
            limits, *queries, *keys, *values, amax
        )
        got = [x_shift(parts[t], -t) for t in (1, 2, 3)]
        o = call(merge_kernel, [((TOK, W), BF16)], n_in=4)(parts[0], *got)[0]
        attended = [o] + [x_shift(o, t) for t in (1, 2, 3)]
        sent = core_swap(project(send_place, attended, wo))
        kept = project(keep_place, attended, wo)
        own_sum, *sends = call(
            core_sum_kernel, [((TOK, 2 * W), F32)] + [((TOK, 2 * W), BF16)] * 3, n_in=2
        )(kept, sent)
        got = [y_shift(sends[s - 1], -s) for s in (1, 2, 3)]
        return call(y_sum_kernel, [((TOK, 2 * W), BF16)], n_in=4)(own_sum, *got)[0]

    base = block_back(pair, 0)
    share = layer(pair, 0)
    total = block_back(share, 0).astype(F32) + block_back(share, 1).astype(F32)
    first = (base.astype(F32) + gate_first * total).astype(BF16)
    second = pick(dest_block == BLOCKS - 1, fresh_pair, first)
    base = turned(pick(zh == 0, second[:, :W], second[:, W:]), 0)
    share = layer(second, 1)
    mine_half = pick(zh == 0, share[:, :W], share[:, W:])
    other_half = pick(zh == 0, share[:, W:], share[:, :W])
    total = turned(mine_half, 0).astype(F32) + turned(other_half, 1).astype(F32)
    return (base.astype(F32) + gate_second * total).astype(BF16)


def solution(mesh):
    return jax.shard_map(
        on_device,
        mesh=mesh,
        in_specs=(
            P("ctx", "head"),
            P(),
            P(None, "ctx", "head"),
            P("head", "ctx"),
            P(),
            P(),
            P(),
            P(),
        ),
        out_specs=P("ctx", "head"),
        check_vma=False,
    )
```

```python
import functools

import jax
import jax.numpy as jnp
from jax import lax
from jax.experimental import pallas as pl
from jax.experimental.pallas import tpu as pltpu
from jax.sharding import PartitionSpec as P

HD = 128
TOK = 128
W = 384
BLOCKS = 16
KEY_BOUND = 8.0
NEG = -1e30
F32 = jnp.float32
BF16 = jnp.bfloat16

BOTH = ("ctx", "head")


def coords():
    return [(x, zl, y, zh, core) for x in range(4) for zl in range(4) for y in range(4) for zh in range(2) for core in range(2)]


def flat(x, zl, y, zh, core):
    return ((x * 4 + zl) * 4 + y) * 4 + zh * 2 + core


def x_shift(a, t):
    return lax.ppermute(a, "ctx", [(c, (c + 4 * t) % 16) for c in range(16)])


def zl_shift(a, t):
    return lax.ppermute(a, "ctx", [(c, c // 4 * 4 + (c + t) % 4) for c in range(16)])


def y_shift(a, t):
    return lax.ppermute(a, "head", [(g, (g + 4 * t) % 16) for g in range(16)])


def head_swap(a, bit):
    return lax.ppermute(a, "head", [(g, g ^ bit) for g in range(16)])


def core_swap(a):
    return head_swap(a, 1)


def turned(a, flip):
    pairs = [(flat(x, zl, y, zh, core), flat(y, zl, x, zh ^ flip, core)) for x, zl, y, zh, core in coords()]
    return lax.ppermute(a, BOTH, pairs)


def block_back(a, flip):
    pairs = []
    for x, zl, y, zh, core in coords():
        to_y, to_zl = divmod((y * 4 + zl + 15) % 16, 4)
        pairs.append((flat(x, zl, y, zh, core), flat(x, to_zl, to_y, zh ^ flip, core)))
    return lax.ppermute(a, BOTH, pairs)


def call(kernel, outs, scratch=(), smem=0, n_in=0, room=6):
    specs = [pl.BlockSpec(memory_space=pltpu.SMEM)] * smem + [pl.BlockSpec(memory_space=pltpu.VMEM)] * n_in
    return pl.pallas_call(
        kernel,
        out_shape=[jax.ShapeDtypeStruct(s, d) for s, d in outs],
        in_specs=specs,
        out_specs=[pl.BlockSpec(memory_space=pltpu.VMEM)] * len(outs),
        scratch_shapes=list(scratch),
        compiler_params=pltpu.CompilerParams(vmem_limit_bytes=room * 1024 * 1024),
    )


def dot(a, b):
    return jnp.dot(a, b, preferred_element_type=F32)


def rounded(a):
    return a.astype(BF16).astype(F32)


def pieces(row):
    high = rounded(row)
    middle = rounded(row - high)
    return jnp.concatenate([high, middle, row - high - middle], axis=1)


def joined(row):
    return row[:, 0:HD] + row[:, HD : 2 * HD] + row[:, 2 * HD : 3 * HD]


SLOT = TOK + 16


def project_in_kernel(parts, place, *refs):
    own, other, mods, weights = refs[0:4], refs[4:8], refs[8], refs[9 : 9 + 4 * parts]
    h_ref, own_out, sends, small = refs[-6], refs[-5], refs[-4:-1], refs[-1]
    turn, zl, core = place[0], place[1], place[2]
    row16 = lax.broadcasted_iota(jnp.int32, (16, W), 0)
    column = lax.broadcasted_iota(jnp.int32, (TOK, 128), 1)
    table = jnp.zeros((TOK, 128), F32)
    for s in range(4):
        start = ((turn - s) & 3) * SLOT
        rows = pl.ds(pl.multiple_of(start, 16), TOK)
        extra = pl.ds(pl.multiple_of(start + TOK, 16), 16)
        total = jnp.zeros((TOK, 1), F32)
        for tiles, at, c in ((own, s, core), (other, 8 + s, 1 - core)):
            scale, shift = mods[at : at + 1, :], mods[at + 4 : at + 5, :]
            tile = tiles[s][...].astype(F32)
            total = total + jnp.sum(tile * tile, axis=1, keepdims=True)
            scaled = (tile * (1.0 + scale)).astype(BF16)
            for half in range(2):
                cols = slice(half * W, (half + 1) * W)
                ring = (zl - (2 * half + c)) & 3
                high = rounded(shift[:, cols])
                low = shift[:, cols] - high
                h_ref[ring, rows, :] = scaled[:, cols]
                h_ref[ring, extra, :] = jnp.where(row16 == 0, high, jnp.where(row16 == 1, low, 0.0)).astype(BF16)
        table = jnp.where(column == s, total, table)
    table = table.T
    for s in range(4):
        small[(turn - s) & 3] = jnp.broadcast_to(table[s : s + 1, :], (8, 128))
    for part in range(parts):
        place_out = slice(part * W, (part + 1) * W)
        w = weights[4 * min(part, 1) : 4 * min(part, 1) + 4]
        w_rows = slice(max(part - 1, 0) * W, (max(part - 1, 0) + 1) * W)
        acc = dot(h_ref[0], w[0][w_rows, :])
        for ring in range(1, 4):
            acc = acc + dot(h_ref[ring], w[ring][w_rows, :])
        own_out[0:TOK, place_out] = acc[0:TOK]
        for t in range(4):
            at = t * SLOT
            tail = acc[at + TOK : at + SLOT]
            if part == 0:
                tail = jnp.where(row16 == 2, pieces(small[t][0:1, :]), tail)
            if t == 0:
                own_out[TOK:SLOT, place_out] = tail
            else:
                sends[t - 1][0:TOK, place_out] = acc[at : at + TOK].astype(BF16)
                sends[t - 1][TOK:SLOT, place_out] = tail.astype(BF16)


def value_query_kernel(h_ref, *refs):
    weights, own_out, sends = refs[0:4], refs[4], refs[5:8]
    for part in range(2):
        cols = slice(part * W, (part + 1) * W)
        acc = dot(h_ref[0], weights[0][cols, :])
        for ring in range(1, 4):
            acc = acc + dot(h_ref[ring], weights[ring][cols, :])
        own_out[:, cols] = acc[0:SLOT]
        for t in range(1, 4):
            sends[t - 1][:, cols] = acc[t * SLOT : (t + 1) * SLOT].astype(BF16)


def key_sum_kernel(own, a, b, c, key_out, norm_out):
    tail = own[TOK:, 0:W] + a[TOK:, 0:W].astype(F32) + b[TOK:, 0:W].astype(F32) + c[TOK:, 0:W].astype(F32)
    r = lax.rsqrt(joined(tail[2:3, :]) * (1.0 / (16 * W)) + 1e-06)
    norm = jnp.broadcast_to(r, (TOK, 128)).T
    norm_out[...] = norm
    tops = jnp.zeros((1, HD), F32)
    for head in range(3):
        cols = slice(head * HD, (head + 1) * HD)
        k = own[0:TOK, cols] + a[0:TOK, cols].astype(F32) + b[0:TOK, cols].astype(F32) + c[0:TOK, cols].astype(F32)
        k = k * norm + (tail[0:1, cols] + tail[1:2, cols])
        key_out[0:TOK, cols] = k.astype(BF16)
        tops = jnp.maximum(tops, jnp.max(jnp.abs(k), axis=0, keepdims=True))
    key_out[TOK:] = jnp.broadcast_to(pieces(tops), (16, W)).astype(BF16)


def summed(own, a, b, c, norm, first):
    out = []
    for head in range(3):
        cols = slice(first + head * HD, first + (head + 1) * HD)
        total = own[:, cols] + a[:, cols].astype(F32) + b[:, cols].astype(F32) + c[:, cols].astype(F32)
        out.append(total[0:TOK] * norm + (total[TOK : TOK + 1] + total[TOK + 1 : TOK + 2]))
    return out


def value_sum_kernel(first, own, a, b, c, norm, out):
    for head, v in enumerate(summed(own, a, b, c, norm[...], first)):
        out[:, head * HD : (head + 1) * HD] = v.astype(BF16)


def largest(tails):
    tops = [joined(t[TOK:, :].astype(F32)[0:1, :]) for t in tails]
    return jnp.maximum(jnp.maximum(tops[0], tops[1]), jnp.maximum(tops[2], tops[3]))


def top_kernel(t0, t1, t2, t3, out):
    out[...] = jnp.broadcast_to(largest([t0, t1, t2, t3]), (8, HD))


def query_sum_kernel(first, own, a, b, c, norm, amax, out):
    for head, q in enumerate(summed(own, a, b, c, norm[...], first)):
        out[0:TOK, head * HD : (head + 1) * HD] = q.astype(BF16)
    out[TOK:] = jnp.broadcast_to(pieces(amax[0:1, :]), (16, W)).astype(BF16)


def attend_kernel(limits, *refs):
    queries, keys, values, outs = refs[0:4], refs[4:8], refs[8:12], refs[12:16]
    factor = KEY_BOUND / (largest(queries) + 1e-06) * HD ** (-0.5)
    column = lax.broadcasted_iota(jnp.int32, (1, 4 * TOK), 1)
    inner = column % TOK
    col128 = lax.broadcasted_iota(jnp.int32, (TOK, 128), 1)
    masks = []
    for t in range(4):
        limit = jnp.zeros((1, 4 * TOK), jnp.int32)
        for u in range(4):
            limit = jnp.where(column // TOK == u, limits[t * 4 + u], limit)
        masks.append(inner < limit)
    stats = [jnp.zeros((TOK, 128), F32) for _ in range(4)]
    for head in range(3):
        cols = slice(head * HD, (head + 1) * HD)
        k = jnp.concatenate([ref[0:TOK, cols] for ref in keys], axis=0)
        v = jnp.concatenate([ref[:, cols] for ref in values], axis=0)
        for t in range(4):
            allowed = jnp.broadcast_to(masks[t], (TOK, 4 * TOK))
            q = (queries[t][0:TOK, cols].astype(F32) * factor).astype(BF16)
            s = lax.dot_general(q, k, (((1,), (1,)), ((), ())), preferred_element_type=F32)
            s = jnp.where(allowed, s, NEG)
            top = jnp.max(s, axis=1, keepdims=True)
            w = jnp.where(allowed, jnp.exp(s - top), 0.0)
            total = jnp.sum(w, axis=1, keepdims=True)
            some = total > 0.0
            safe = jnp.where(some, total, 1.0)
            outs[t][:, cols] = (dot(w.astype(BF16), v) / safe).astype(BF16)
            lse = jnp.where(some, top + jnp.log(safe), NEG)
            for piece in range(3):
                part = rounded(lse)
                stats[t] = jnp.where(col128 == head * 3 + piece, part, stats[t])
                lse = lse - part
    for t in range(4):
        outs[t][:, W:] = stats[t].astype(BF16)


def merge_kernel(*refs):
    parts, out = refs[0:4], refs[4]
    stats = [p[:, W:].astype(F32) for p in parts]
    for head in range(3):
        cols = slice(head * HD, (head + 1) * HD)
        at = head * 3
        lse = [s[:, at : at + 1] + s[:, at + 1 : at + 2] + s[:, at + 2 : at + 3] for s in stats]
        top = jnp.maximum(jnp.maximum(lse[0], lse[1]), jnp.maximum(lse[2], lse[3]))
        share = [jnp.exp(e - top) for e in lse]
        acc = share[0] * parts[0][:, cols].astype(F32)
        for i in range(1, 4):
            acc = acc + share[i] * parts[i][:, cols].astype(F32)
        out[:, cols] = (acc / (share[0] + share[1] + share[2] + share[3])).astype(BF16)


def project_kernel(place, *refs):
    attended, weights, out, o_all, w_all = refs[0:4], refs[4:8], refs[8], refs[9], refs[10]
    turn, zl, parity = place[0], place[1], place[2]
    for t in range(4):
        o_all[t] = attended[t][...]
        w_all[t] = weights[t][...]
    rows = jnp.concatenate([o_all[(turn + s) & 3] for s in range(4)], axis=0)
    for half in range(2):
        ring = (zl - (2 * half + parity)) & 3
        out[:, half * W : (half + 1) * W] = dot(rows, w_all[ring]).astype(BF16)


def project(place, attended, weights):
    return call(
        project_kernel,
        [((4 * TOK, 2 * W), BF16)],
        scratch=[pltpu.VMEM((4, TOK, W), BF16), pltpu.VMEM((4, W, W), BF16)],
        smem=1,
        n_in=8,
        room=10,
    )(place, *attended, *weights)[0]


def core_sum_kernel(a, b, own, *sends):
    own[...] = a[0:TOK].astype(F32) + b[0:TOK].astype(F32)
    for s in range(1, 4):
        rows = slice(s * TOK, (s + 1) * TOK)
        sends[s - 1][...] = (a[rows].astype(F32) + b[rows].astype(F32)).astype(BF16)


def y_sum_kernel(own, a, b, c, out):
    out[...] = (own[...] + a[...].astype(F32) + b[...].astype(F32) + c[...].astype(F32)).astype(BF16)


def after(a, dep):
    return lax.optimization_barrier((a, dep))[0]


def pick(flag, a, b):
    return jnp.where(flag, a, b)


def on_device(hidden, fresh, w_qkv, w_out, mod_table, levels, block_mask, counts):
    ctx_at = lax.axis_index("ctx")
    head_at = lax.axis_index("head")
    x, zl = ctx_at // 4, ctx_at % 4
    y, zh, core = head_at // 4, (head_at // 2) % 2, head_at % 2
    four = jnp.arange(4, dtype=jnp.int32)
    ids = jnp.arange(BLOCKS, dtype=jnp.int32)

    a0, a1 = turned(hidden, 0), turned(hidden, 1)
    pair = pick(zh == 0, jnp.concatenate([a0, a1], 1), jnp.concatenate([a1, a0], 1))

    w_k = [w_qkv[1]]
    w_vq = jnp.concatenate([w_qkv[2], w_qkv[0]], 0)
    w_k.append(zl_shift(w_k[0], 1))

    chunks = [(x * 4 + 2 * half + c) * W for c in (core, 1 - core) for half in (0, 1)]
    mod_chunks = [lax.dynamic_slice_in_dim(mod_table, at, W, 2) for at in chunks]
    mod_own = jnp.concatenate(mod_chunks[:2], 2)
    mod_other = jnp.concatenate(mod_chunks[2:], 2)
    level_ids = jnp.arange(mod_table.shape[1], dtype=jnp.int32)

    def rows_at(table, level):
        hot = level[..., None] == level_ids
        return jnp.sum(jnp.where(hot[..., None], table, 0.0), axis=-2)

    def level_of(step, blocks):
        return jnp.sum(jnp.where(blocks[..., None] == ids, levels[step], 0), axis=-1)

    slot_blocks = (y - four) % 4 * 4 + zl
    dest_block = y * 4 + zl
    gate_first = rows_at(mod_own[2], level_of(0, dest_block + 1))
    own_cols = lax.dynamic_slice_in_dim(mod_table[2], head_at * W, W, 1)
    gate_second = rows_at(own_cols, level_of(1, ctx_at))
    fresh_pair = jnp.concatenate([lax.dynamic_slice_in_dim(fresh, at, W, 1) for at in chunks[:2]], 1)

    key_place = jnp.stack([(y - x) % 4, zl, core]).astype(jnp.int32)
    keep_place = jnp.stack([(x - y) % 4, zl, core]).astype(jnp.int32)
    send_place = jnp.stack([(x - y) % 4, zl, 1 - core]).astype(jnp.int32)
    query_blocks = (x - four) % 4 * 4 + zl
    key_blocks = x * 4 + (zl - four) % 4
    seen = jnp.sum(jnp.where((query_blocks[:, None] == ids)[..., None], block_mask, 0), axis=1)
    seen = jnp.sum(jnp.where(key_blocks[:, None] == ids, seen[:, None, :], 0), axis=-1)

    def small_for(step):
        lv = level_of(step, slot_blocks)
        mods = jnp.concatenate([rows_at(m[k], lv) for m in (mod_own, mod_other) for k in (1, 0)], 0)
        live = jnp.sum(jnp.where(key_blocks[:, None] == ids, counts[step : step + BLOCKS], 0), axis=-1)
        return mods, (seen * live).reshape(16).astype(jnp.int32)

    smalls = [small_for(step) for step in range(2)]
    pair, w_vq, smalls, gate_first, gate_second, fresh_pair = lax.optimization_barrier(
        (pair, w_vq, smalls, gate_first, gate_second, fresh_pair)
    )
    w_vq = [w_vq, zl_shift(w_vq, 1)]
    w_k.append(zl_shift(w_k[1], 1))
    w_k.append(zl_shift(w_k[2], 1))
    w_o = [w_out]
    moved = []

    def more(ring, dep):
        ring.append(zl_shift(after(ring[-1], dep), 1))

    def layer(pair, step):
        mods, limits = smalls[step]
        own = [pair] + [y_shift(pair, s) for s in (1, 2, 3)]
        other = [core_swap(a) for a in own]
        parts = 1 if step == 0 else 3
        h, k_own, *k_sends = call(
            functools.partial(project_in_kernel, parts),
            [((4, 4 * SLOT, W), BF16), ((SLOT, parts * W), F32)] + [((SLOT, parts * W), BF16)] * 3,
            scratch=[pltpu.VMEM((4, 8, 128), F32)],
            smem=1,
            n_in=13 if step == 0 else 17,
            room=16,
        )(key_place, *own, *other, mods, *w_k, *(w_vq if step else []))
        if step == 0:
            more(w_vq, h)
        k_got = [x_shift(k_sends[t - 1], t) for t in (1, 2, 3)]
        k_c, norm = call(key_sum_kernel, [((SLOT, W), BF16), ((TOK, 128), F32)], n_in=4)(k_own, *k_got)
        keys = [k_c] + [zl_shift(k_c, u) for u in (1, 2, 3)]
        if step == 0:
            more(w_vq, k_c)
        amax = call(top_kernel, [((8, HD), F32)], n_in=4)(*keys)[0]
        amax = jnp.maximum(amax, head_swap(amax, 1))
        amax = jnp.maximum(amax, head_swap(amax, 2))
        near = amax
        amax = jnp.maximum(amax, head_swap(amax, 4))
        amax = jnp.maximum(amax, head_swap(amax, 8))
        if step == 0:
            vq_own, *vq_sends = call(
                value_query_kernel,
                [((SLOT, 2 * W), F32)] + [((SLOT, 2 * W), BF16)] * 3,
                n_in=5,
                room=16,
            )(after(h, amax), *w_vq)
            more(w_o, w_vq[3])
            vq_got = [x_shift(vq_sends[t - 1], t) for t in (1, 2, 3)]
        else:
            vq_own, vq_got = k_own, k_got
        at = step * W
        v_c = call(functools.partial(value_sum_kernel, at), [((TOK, W), BF16)], n_in=5)(vq_own, *vq_got, norm)[0]
        v_c = after(v_c, near)
        values = [v_c] + [zl_shift(v_c, u) for u in (1, 2, 3)]
        q_b = call(functools.partial(query_sum_kernel, at + W), [((SLOT, W), BF16)], n_in=6)(
            vq_own, *vq_got, norm, amax
        )[0]
        queries = [q_b] + [x_shift(q_b, t) for t in (1, 2, 3)]
        if step == 0:
            more(w_o, v_c)
            moved.append(block_back(after(pair, queries[1]), 0))
        parts = call(attend_kernel, [((TOK, W + 128), BF16)] * 4, smem=1, n_in=12, room=12)(
            limits, *queries, *keys, *values
        )
        got = [x_shift(parts[t], -t) for t in (1, 2, 3)]
        o = call(merge_kernel, [((TOK, W), BF16)], n_in=4)(parts[0], *got)[0]
        if step == 0:
            more(w_o, parts[0])
            o, moved[0] = lax.optimization_barrier((o, moved[0]))
        attended = [o] + [x_shift(o, t) for t in (1, 2, 3)]
        sent = core_swap(project(send_place, attended, w_o))
        kept = project(keep_place, attended, w_o)
        own_sum, *sends = call(
            core_sum_kernel, [((TOK, 2 * W), F32)] + [((TOK, 2 * W), BF16)] * 3, n_in=2
        )(kept, sent)
        got = [y_shift(sends[s - 1], -s) for s in (1, 2, 3)]
        return call(y_sum_kernel, [((TOK, 2 * W), BF16)], n_in=4)(own_sum, *got)[0]

    share = layer(pair, 0)
    base = moved[0]
    total = block_back(share, 0).astype(F32) + block_back(share, 1).astype(F32)
    first = (base.astype(F32) + gate_first * total).astype(BF16)
    second = pick(dest_block == BLOCKS - 1, fresh_pair, first)
    base = turned(pick(zh == 0, second[:, :W], second[:, W:]), 0)
    share = layer(second, 1)
    mine_half = pick(zh == 0, share[:, :W], share[:, W:])
    other_half = pick(zh == 0, share[:, W:], share[:, :W])
    total = turned(mine_half, 0).astype(F32) + turned(other_half, 1).astype(F32)
    return (base.astype(F32) + gate_second * total).astype(BF16)


def solution(mesh):
    return jax.shard_map(
        on_device,
        mesh=mesh,
        in_specs=(
            P("ctx", "head"),
            P(),
            P(None, "ctx", "head"),
            P("head", "ctx"),
            P(),
            P(),
            P(),
            P(),
        ),
        out_specs=P("ctx", "head"),
        check_vma=False,
    )
```

```python
import functools

import jax
import jax.numpy as jnp
from jax import lax
from jax.experimental import pallas as pl
from jax.experimental.pallas import tpu as pltpu
from jax.sharding import PartitionSpec as P

HD = 128
TOK = 128
W = 384
BLOCKS = 16
KEY_BOUND = 8.0
NEG = -1e30
F32 = jnp.float32
BF16 = jnp.bfloat16

BOTH = ("ctx", "head")


def coords():
    return [(x, zl, y, zh, core) for x in range(4) for zl in range(4) for y in range(4) for zh in range(2) for core in range(2)]


def flat(x, zl, y, zh, core):
    return ((x * 4 + zl) * 4 + y) * 4 + zh * 2 + core


def x_shift(a, t):
    return lax.ppermute(a, "ctx", [(c, (c + 4 * t) % 16) for c in range(16)])


def zl_shift(a, t):
    return lax.ppermute(a, "ctx", [(c, c // 4 * 4 + (c + t) % 4) for c in range(16)])


def y_shift(a, t):
    return lax.ppermute(a, "head", [(g, (g + 4 * t) % 16) for g in range(16)])


def head_swap(a, bit):
    return lax.ppermute(a, "head", [(g, g ^ bit) for g in range(16)])


def core_swap(a):
    return head_swap(a, 1)


def turned(a, flip):
    pairs = [(flat(x, zl, y, zh, core), flat(y, zl, x, zh ^ flip, core)) for x, zl, y, zh, core in coords()]
    return lax.ppermute(a, BOTH, pairs)


def block_back(a, flip):
    pairs = []
    for x, zl, y, zh, core in coords():
        to_y, to_zl = divmod((y * 4 + zl + 15) % 16, 4)
        pairs.append((flat(x, zl, y, zh, core), flat(x, to_zl, to_y, zh ^ flip, core)))
    return lax.ppermute(a, BOTH, pairs)


def call(kernel, outs, scratch=(), smem=0, n_in=0, n_far=0, room=6):
    specs = [pl.BlockSpec(memory_space=pltpu.SMEM)] * smem + [pl.BlockSpec(memory_space=pltpu.VMEM)] * n_in
    specs += [pl.BlockSpec(memory_space=pltpu.HBM)] * n_far
    return pl.pallas_call(
        kernel,
        out_shape=[jax.ShapeDtypeStruct(s, d) for s, d in outs],
        in_specs=specs,
        out_specs=[pl.BlockSpec(memory_space=pltpu.VMEM)] * len(outs),
        scratch_shapes=list(scratch),
        compiler_params=pltpu.CompilerParams(vmem_limit_bytes=room * 1024 * 1024),
    )


def dot(a, b):
    return jnp.dot(a, b, preferred_element_type=F32)


def rounded(a):
    return a.astype(BF16).astype(F32)


def pieces(row):
    high = rounded(row)
    middle = rounded(row - high)
    return jnp.concatenate([high, middle, row - high - middle], axis=1)


def joined(row):
    return row[:, 0:HD] + row[:, HD : 2 * HD] + row[:, 2 * HD : 3 * HD]


SLOT = TOK + 16


def build(place, mods, tiles, h_ref, small):
    turn, zl, core = place[0], place[1], place[2]
    row16 = lax.broadcasted_iota(jnp.int32, (16, W), 0)
    column = lax.broadcasted_iota(jnp.int32, (TOK, 128), 1)
    table = jnp.zeros((TOK, 128), F32)
    for s in range(4):
        start = ((turn - s) & 3) * SLOT
        rows = pl.ds(pl.multiple_of(start, 16), TOK)
        extra = pl.ds(pl.multiple_of(start + TOK, 16), 16)
        total = jnp.zeros((TOK, 1), F32)
        for tile_ref, at, c in ((tiles[s], s, core), (tiles[4 + s], 8 + s, 1 - core)):
            scale, shift = mods[at : at + 1, :], mods[at + 4 : at + 5, :]
            tile = tile_ref[...].astype(F32)
            total = total + jnp.sum(tile * tile, axis=1, keepdims=True)
            scaled = (tile * (1.0 + scale)).astype(BF16)
            for half in range(2):
                cols = slice(half * W, (half + 1) * W)
                ring = (zl - (2 * half + c)) & 3
                high = rounded(shift[:, cols])
                low = shift[:, cols] - high
                h_ref[ring, rows, :] = scaled[:, cols]
                h_ref[ring, extra, :] = jnp.where(row16 == 0, high, jnp.where(row16 == 1, low, 0.0)).astype(BF16)
        table = jnp.where(column == s, total, table)
    table = table.T
    for s in range(4):
        small[(turn - s) & 3] = jnp.broadcast_to(table[s : s + 1, :], (8, 128))


def multiply(h_ref, small, weight, own_out, sends):
    row16 = lax.broadcasted_iota(jnp.int32, (16, W), 0)
    acc = None
    for ring in range(4):
        term = dot(h_ref[ring], weight(ring))
        acc = term if acc is None else acc + term
    for t in range(4):
        at = t * SLOT
        tail = jnp.where(row16 == 2, pieces(small[t][0:1, :]), acc[at + TOK : at + SLOT])
        if t == 0:
            own_out[0:TOK] = acc[0:TOK]
            own_out[TOK:SLOT] = tail
        else:
            sends[t - 1][0:TOK] = acc[at : at + TOK].astype(BF16)
            sends[t - 1][TOK:SLOT] = tail.astype(BF16)


def build_kernel(place, mods, *refs):
    build(place, mods, refs[0:8], refs[8], refs[9])


def key_kernel(h_ref, small, *refs):
    multiply(h_ref, small, lambda ring: refs[ring][...], refs[4], refs[5:8])


def build_key_kernel(place, mods, *refs):
    tiles, far, h_ref, own_out, sends, small, weights, sems = refs[0:8], refs[8:12], refs[12], refs[13], refs[14:17], refs[17], refs[18], refs[19]
    copies = [pltpu.make_async_copy(far[i], weights.at[i], sems.at[i]) for i in range(4)]
    for copy in copies:
        copy.start()
    build(place, mods, tiles, h_ref, small)
    for copy in copies:
        copy.wait()
    multiply(h_ref, small, lambda ring: weights[ring], own_out, sends)


def value_query_kernel(h_ref, *refs):
    weights, own_out, sends = refs[0:4], refs[4], refs[5:8]
    for part in range(2):
        cols = slice(part * W, (part + 1) * W)
        acc = dot(h_ref[0], weights[0][cols, :])
        for ring in range(1, 4):
            acc = acc + dot(h_ref[ring], weights[ring][cols, :])
        own_out[:, cols] = acc[0:SLOT]
        for t in range(1, 4):
            sends[t - 1][:, cols] = acc[t * SLOT : (t + 1) * SLOT].astype(BF16)


def key_sum_kernel(own, a, b, c, key_out, norm_out):
    tail = own[TOK:, 0:W] + a[TOK:, 0:W].astype(F32) + b[TOK:, 0:W].astype(F32) + c[TOK:, 0:W].astype(F32)
    r = lax.rsqrt(joined(tail[2:3, :]) * (1.0 / (16 * W)) + 1e-06)
    norm = jnp.broadcast_to(r, (TOK, 128)).T
    norm_out[...] = norm
    tops = jnp.zeros((1, HD), F32)
    for head in range(3):
        cols = slice(head * HD, (head + 1) * HD)
        k = own[0:TOK, cols] + a[0:TOK, cols].astype(F32) + b[0:TOK, cols].astype(F32) + c[0:TOK, cols].astype(F32)
        k = k * norm + (tail[0:1, cols] + tail[1:2, cols])
        key_out[0:TOK, cols] = k.astype(BF16)
        tops = jnp.maximum(tops, jnp.max(jnp.abs(k), axis=0, keepdims=True))
    key_out[TOK:] = jnp.broadcast_to(pieces(tops), (16, W)).astype(BF16)


def summed(own, a, b, c, norm, first):
    out = []
    for head in range(3):
        cols = slice(first + head * HD, first + (head + 1) * HD)
        total = own[:, cols] + a[:, cols].astype(F32) + b[:, cols].astype(F32) + c[:, cols].astype(F32)
        out.append(total[0:TOK] * norm + (total[TOK : TOK + 1] + total[TOK + 1 : TOK + 2]))
    return out


def value_sum_kernel(first, own, a, b, c, norm, out):
    for head, v in enumerate(summed(own, a, b, c, norm[...], first)):
        out[:, head * HD : (head + 1) * HD] = v.astype(BF16)


def largest(tails):
    tops = [joined(t[TOK:, :].astype(F32)[0:1, :]) for t in tails]
    return jnp.maximum(jnp.maximum(tops[0], tops[1]), jnp.maximum(tops[2], tops[3]))


def top_kernel(t0, t1, t2, t3, out):
    out[...] = jnp.broadcast_to(largest([t0, t1, t2, t3]), (8, HD))


def query_sum_kernel(first, own, a, b, c, norm, amax, out):
    for head, q in enumerate(summed(own, a, b, c, norm[...], first)):
        out[0:TOK, head * HD : (head + 1) * HD] = q.astype(BF16)
    out[TOK:] = jnp.broadcast_to(pieces(amax[0:1, :]), (16, W)).astype(BF16)


def attend_kernel(limits, *refs):
    queries, keys, values, outs = refs[0:4], refs[4:8], refs[8:12], refs[12:16]
    factor = KEY_BOUND / (largest(queries) + 1e-06) * HD ** (-0.5)
    column = lax.broadcasted_iota(jnp.int32, (1, 4 * TOK), 1)
    inner = column % TOK
    col128 = lax.broadcasted_iota(jnp.int32, (TOK, 128), 1)
    masks = []
    for t in range(4):
        limit = jnp.zeros((1, 4 * TOK), jnp.int32)
        for u in range(4):
            limit = jnp.where(column // TOK == u, limits[t * 4 + u], limit)
        masks.append(inner < limit)
    stats = [jnp.zeros((TOK, 128), F32) for _ in range(4)]
    for head in range(3):
        cols = slice(head * HD, (head + 1) * HD)
        k = jnp.concatenate([ref[0:TOK, cols] for ref in keys], axis=0)
        v = jnp.concatenate([ref[:, cols] for ref in values], axis=0)
        for t in range(4):
            allowed = jnp.broadcast_to(masks[t], (TOK, 4 * TOK))
            q = (queries[t][0:TOK, cols].astype(F32) * factor).astype(BF16)
            s = lax.dot_general(q, k, (((1,), (1,)), ((), ())), preferred_element_type=F32)
            s = jnp.where(allowed, s, NEG)
            top = jnp.max(s, axis=1, keepdims=True)
            w = jnp.where(allowed, jnp.exp(s - top), 0.0)
            total = jnp.sum(w, axis=1, keepdims=True)
            some = total > 0.0
            safe = jnp.where(some, total, 1.0)
            outs[t][:, cols] = (dot(w.astype(BF16), v) / safe).astype(BF16)
            lse = jnp.where(some, top + jnp.log(safe), NEG)
            for piece in range(3):
                part = rounded(lse)
                stats[t] = jnp.where(col128 == head * 3 + piece, part, stats[t])
                lse = lse - part
    for t in range(4):
        outs[t][:, W:] = stats[t].astype(BF16)


def merge_kernel(*refs):
    parts, out = refs[0:4], refs[4]
    stats = [p[:, W:].astype(F32) for p in parts]
    for head in range(3):
        cols = slice(head * HD, (head + 1) * HD)
        at = head * 3
        lse = [s[:, at : at + 1] + s[:, at + 1 : at + 2] + s[:, at + 2 : at + 3] for s in stats]
        top = jnp.maximum(jnp.maximum(lse[0], lse[1]), jnp.maximum(lse[2], lse[3]))
        share = [jnp.exp(e - top) for e in lse]
        acc = share[0] * parts[0][:, cols].astype(F32)
        for i in range(1, 4):
            acc = acc + share[i] * parts[i][:, cols].astype(F32)
        out[:, cols] = (acc / (share[0] + share[1] + share[2] + share[3])).astype(BF16)


def project_kernel(place, *refs):
    attended, weights, out, o_all, w_all = refs[0:4], refs[4:8], refs[8], refs[9], refs[10]
    turn, zl, parity = place[0], place[1], place[2]
    for t in range(4):
        o_all[t] = attended[t][...]
        w_all[t] = weights[t][...]
    rows = jnp.concatenate([o_all[(turn + s) & 3] for s in range(4)], axis=0)
    for half in range(2):
        ring = (zl - (2 * half + parity)) & 3
        out[:, half * W : (half + 1) * W] = dot(rows, w_all[ring]).astype(BF16)


def project(place, attended, weights):
    return call(
        project_kernel,
        [((4 * TOK, 2 * W), BF16)],
        scratch=[pltpu.VMEM((4, TOK, W), BF16), pltpu.VMEM((4, W, W), BF16)],
        smem=1,
        n_in=8,
        room=10,
    )(place, *attended, *weights)[0]


def core_sum_kernel(a, b, own, *sends):
    own[...] = a[0:TOK].astype(F32) + b[0:TOK].astype(F32)
    for s in range(1, 4):
        rows = slice(s * TOK, (s + 1) * TOK)
        sends[s - 1][...] = (a[rows].astype(F32) + b[rows].astype(F32)).astype(BF16)


def y_sum_kernel(own, a, b, c, gate, keep, base, out):
    total = own[...] + a[...].astype(F32) + b[...].astype(F32) + c[...].astype(F32)
    out[...] = (total * gate[...] + base[...].astype(F32) * keep[...]).astype(BF16)


def after(a, dep):
    return lax.optimization_barrier((a, dep))[0]


def pick(flag, a, b):
    return jnp.where(flag, a, b)


def on_device(hidden, fresh, w_qkv, w_out, mod_table, levels, block_mask, counts):
    ctx_at = lax.axis_index("ctx")
    head_at = lax.axis_index("head")
    x, zl = ctx_at // 4, ctx_at % 4
    y, zh, core = head_at // 4, (head_at // 2) % 2, head_at % 2
    four = jnp.arange(4, dtype=jnp.int32)
    ids = jnp.arange(BLOCKS, dtype=jnp.int32)

    a0, a1 = turned(hidden, 0), turned(hidden, 1)
    pair = pick(zh == 0, jnp.concatenate([a0, a1], 1), jnp.concatenate([a1, a0], 1))

    w_k = [w_qkv[1], zl_shift(w_qkv[1], 1), zl_shift(w_qkv[1], 3)]
    w_vq = jnp.concatenate([w_qkv[2], w_qkv[0]], 0)

    chunks = [(x * 4 + 2 * half + c) * W for c in (core, 1 - core) for half in (0, 1)]
    mod_chunks = [lax.dynamic_slice_in_dim(mod_table, at, W, 2) for at in chunks]
    mod_own = jnp.concatenate(mod_chunks[:2], 2)
    mod_other = jnp.concatenate(mod_chunks[2:], 2)
    level_ids = jnp.arange(mod_table.shape[1], dtype=jnp.int32)

    def rows_at(table, level):
        hot = level[..., None] == level_ids
        return jnp.sum(jnp.where(hot[..., None], table, 0.0), axis=-2)

    def level_of(step, blocks):
        return jnp.sum(jnp.where(blocks[..., None] == ids, levels[step], 0), axis=-1)

    slot_blocks = (y - four) % 4 * 4 + zl
    dest_block = y * 4 + zl
    fresh_pair = jnp.concatenate([lax.dynamic_slice_in_dim(fresh, at, W, 1) for at in chunks[:2]], 1)

    key_place = jnp.stack([(y - x) % 4, zl, core]).astype(jnp.int32)
    keep_place = jnp.stack([(x - y) % 4, zl, core]).astype(jnp.int32)
    send_place = jnp.stack([(x - y) % 4, zl, 1 - core]).astype(jnp.int32)
    query_blocks = (x - four) % 4 * 4 + zl
    key_blocks = x * 4 + (zl - four) % 4
    seen = jnp.sum(jnp.where((query_blocks[:, None] == ids)[..., None], block_mask, 0), axis=1)
    seen = jnp.sum(jnp.where(key_blocks[:, None] == ids, seen[:, None, :], 0), axis=-1)

    def small_for(step):
        lv = level_of(step, slot_blocks)
        mods = jnp.concatenate([rows_at(m[k], lv) for m in (mod_own, mod_other) for k in (1, 0)], 0)
        live = jnp.sum(jnp.where(key_blocks[:, None] == ids, counts[step : step + BLOCKS], 0), axis=-1)
        gate = rows_at(mod_own[2], level_of(step, dest_block))[None]
        half = jnp.arange(2 * W, dtype=jnp.int32)[None] // W
        keep = jnp.where(zh == (half if step else 0), 1.0, 0.0) + jnp.zeros((1, 2 * W), F32)
        return mods, (seen * live).reshape(16).astype(jnp.int32), gate, keep

    smalls = [small_for(step) for step in range(2)]
    pair, w_k, smalls, fresh_pair = lax.optimization_barrier((pair, w_k, smalls, fresh_pair))
    w_k.insert(2, zl_shift(w_k[1], 1))
    w_vq = after(w_vq, w_k[2])
    w_vq = [w_vq, zl_shift(w_vq, 1), zl_shift(w_vq, 3)]
    w_o = [w_out]

    def forward(ring, dep):
        ring.insert(2, zl_shift(after(ring[1], dep), 1))

    def layer(pair, step):
        mods, limits, gate, keep = smalls[step]
        own = [pair] + [y_shift(pair, s) for s in (1, 2, 3)]
        other = [core_swap(a) for a in own]
        h_type, key_types = ((4, 4 * SLOT, W), BF16), [((SLOT, W), F32)] + [((SLOT, W), BF16)] * 3
        if step == 0:
            h, small = call(build_kernel, [h_type, ((4, 8, 128), F32)], smem=1, n_in=9, room=10)(
                key_place, mods, *own, *other
            )
            k_own, *k_sends = call(key_kernel, key_types, n_in=6, room=10)(h, small, *w_k)
        else:
            h, k_own, *k_sends = call(
                build_key_kernel,
                [h_type] + key_types,
                scratch=[pltpu.VMEM((4, 8, 128), F32), pltpu.VMEM((4, W, W), BF16), pltpu.SemaphoreType.DMA((4,))],
                smem=1,
                n_in=9,
                n_far=4,
                room=16,
            )(key_place, mods, *own, *other, *w_k)
        k_got = [x_shift(k_sends[t - 1], t) for t in (1, 2, 3)]
        k_c, norm = call(key_sum_kernel, [((SLOT, W), BF16), ((TOK, 128), F32)], n_in=4)(k_own, *k_got)
        keys = [k_c] + [zl_shift(k_c, u) for u in (1, 2, 3)]
        if step == 0:
            forward(w_vq, k_c)
        amax = call(top_kernel, [((8, HD), F32)], n_in=4)(*keys)[0]
        amax = jnp.maximum(amax, head_swap(amax, 1))
        amax = jnp.maximum(amax, head_swap(amax, 2))
        near = amax
        amax = jnp.maximum(amax, head_swap(amax, 4))
        amax = jnp.maximum(amax, head_swap(amax, 8))
        vq_own, *vq_sends = call(
            value_query_kernel,
            [((SLOT, 2 * W), F32)] + [((SLOT, 2 * W), BF16)] * 3,
            n_in=5,
            room=16,
        )(after(h, keys[1]) if step == 0 else h, *w_vq)
        if step == 1:
            *vq_sends, _ = lax.optimization_barrier((*vq_sends, k_c))
        vq_got = [x_shift(vq_sends[t - 1], t) for t in (1, 2, 3)]
        v_c = call(functools.partial(value_sum_kernel, 0), [((TOK, W), BF16)], n_in=5)(vq_own, *vq_got, norm)[0]
        v_c = after(v_c, near)
        values = [v_c] + [zl_shift(v_c, u) for u in (1, 2, 3)]
        if step == 0:
            start = after(w_out, near)
            w_o.extend([zl_shift(start, 1), zl_shift(start, 3)])
        q_b = call(functools.partial(query_sum_kernel, W), [((SLOT, W), BF16)], n_in=6)(
            vq_own, *vq_got, norm, amax
        )[0]
        queries = [q_b] + [x_shift(q_b, t) for t in (1, 2, 3)]
        parts = call(attend_kernel, [((TOK, W + 128), BF16)] * 4, smem=1, n_in=12, room=12)(
            limits, *queries, *keys, *values
        )
        got = [x_shift(parts[t], -t) for t in (1, 2, 3)]
        o = call(merge_kernel, [((TOK, W), BF16)], n_in=4)(parts[0], *got)[0]
        if step == 0:
            forward(w_o, parts[0])
        attended = [o] + [x_shift(o, t) for t in (1, 2, 3)]
        sent = core_swap(project(send_place, attended, w_o))
        kept = project(keep_place, attended, w_o)
        own_sum, *sends = call(
            core_sum_kernel, [((TOK, 2 * W), F32)] + [((TOK, 2 * W), BF16)] * 3, n_in=2
        )(kept, sent)
        got = [y_shift(sends[s - 1], -s) for s in (1, 2, 3)]
        return call(y_sum_kernel, [((TOK, 2 * W), BF16)], n_in=7)(own_sum, *got, gate, keep, pair)[0]

    share = layer(pair, 0)
    first = (block_back(share, 0).astype(F32) + block_back(share, 1).astype(F32)).astype(BF16)
    second = pick(dest_block == BLOCKS - 1, fresh_pair, first)
    share = layer(second, 1)
    mine_half = pick(zh == 0, share[:, :W], share[:, W:])
    other_half = pick(zh == 0, share[:, W:], share[:, :W])
    return (turned(mine_half, 0).astype(F32) + turned(other_half, 1).astype(F32)).astype(BF16)


def solution(mesh):
    return jax.shard_map(
        on_device,
        mesh=mesh,
        in_specs=(
            P("ctx", "head"),
            P(),
            P(None, "ctx", "head"),
            P("head", "ctx"),
            P(),
            P(),
            P(),
            P(),
        ),
        out_specs=P("ctx", "head"),
        check_vma=False,
    )
```

```python
import functools

import jax
import jax.numpy as jnp
from jax import lax
from jax.experimental import pallas as pl
from jax.experimental.pallas import tpu as pltpu
from jax.sharding import PartitionSpec as P

HD = 128
TOK = 128
W = 384
BLOCKS = 16
KEY_BOUND = 8.0
NEG = -1e30
F32 = jnp.float32
BF16 = jnp.bfloat16

BOTH = ("ctx", "head")


def coords():
    return [(x, zl, y, zh, core) for x in range(4) for zl in range(4) for y in range(4) for zh in range(2) for core in range(2)]


def flat(x, zl, y, zh, core):
    return ((x * 4 + zl) * 4 + y) * 4 + zh * 2 + core


def x_shift(a, t):
    return lax.ppermute(a, "ctx", [(c, (c + 4 * t) % 16) for c in range(16)])


def zl_shift(a, t):
    return lax.ppermute(a, "ctx", [(c, c // 4 * 4 + (c + t) % 4) for c in range(16)])


def y_shift(a, t):
    return lax.ppermute(a, "head", [(g, (g + 4 * t) % 16) for g in range(16)])


def head_swap(a, bit):
    return lax.ppermute(a, "head", [(g, g ^ bit) for g in range(16)])


def core_swap(a):
    return head_swap(a, 1)


def turned(a, flip, back=0):
    pairs = []
    for x, zl, y, zh, core in coords():
        to_x, to_zl = divmod((y * 4 + zl - back) % BLOCKS, 4)
        pairs.append((flat(x, zl, y, zh, core), flat(to_x, to_zl, x, zh ^ flip, core)))
    return lax.ppermute(a, BOTH, pairs)


def call(kernel, outs, scratch=(), smem=0, n_in=0, n_far=0, room=6):
    specs = [pl.BlockSpec(memory_space=pltpu.SMEM)] * smem + [pl.BlockSpec(memory_space=pltpu.VMEM)] * n_in
    specs += [pl.BlockSpec(memory_space=pltpu.HBM)] * n_far
    return pl.pallas_call(
        kernel,
        out_shape=[jax.ShapeDtypeStruct(s, d) for s, d in outs],
        in_specs=specs,
        out_specs=[pl.BlockSpec(memory_space=pltpu.VMEM)] * len(outs),
        scratch_shapes=list(scratch),
        compiler_params=pltpu.CompilerParams(vmem_limit_bytes=room * 1024 * 1024),
    )


def dot(a, b):
    return jnp.dot(a, b, preferred_element_type=F32)


def rounded(a):
    return a.astype(BF16).astype(F32)


def pieces(row):
    high = rounded(row)
    middle = rounded(row - high)
    return jnp.concatenate([high, middle, row - high - middle], axis=1)


def joined(row):
    return row[:, 0:HD] + row[:, HD : 2 * HD] + row[:, 2 * HD : 3 * HD]


SLOT = TOK + 16


def build(place, mods, tiles, h_ref, small):
    turn, zl, core = place[0], place[1], place[2]
    row16 = lax.broadcasted_iota(jnp.int32, (16, W), 0)
    column = lax.broadcasted_iota(jnp.int32, (TOK, 128), 1)
    table = jnp.zeros((TOK, 128), F32)
    for s in range(4):
        start = ((turn - s) & 3) * SLOT
        rows = pl.ds(pl.multiple_of(start, 16), TOK)
        extra = pl.ds(pl.multiple_of(start + TOK, 16), 16)
        total = jnp.zeros((TOK, 1), F32)
        for tile_ref, at, c in ((tiles[s], s, core), (tiles[4 + s], 8 + s, 1 - core)):
            scale, shift = mods[at : at + 1, :], mods[at + 4 : at + 5, :]
            tile = tile_ref[...].astype(F32)
            total = total + jnp.sum(tile * tile, axis=1, keepdims=True)
            scaled = (tile * (1.0 + scale)).astype(BF16)
            for half in range(2):
                cols = slice(half * W, (half + 1) * W)
                ring = (zl - (2 * half + c)) & 3
                high = rounded(shift[:, cols])
                low = shift[:, cols] - high
                h_ref[ring, rows, :] = scaled[:, cols]
                h_ref[ring, extra, :] = jnp.where(row16 == 0, high, jnp.where(row16 == 1, low, 0.0)).astype(BF16)
        table = jnp.where(column == s, total, table)
    table = table.T
    for s in range(4):
        small[(turn - s) & 3] = jnp.broadcast_to(table[s : s + 1, :], (8, 128))


def multiply(h_ref, small, weight, own_out, sends):
    row16 = lax.broadcasted_iota(jnp.int32, (16, W), 0)
    acc = None
    for ring in range(4):
        term = dot(h_ref[ring], weight(ring))
        acc = term if acc is None else acc + term
    for t in range(4):
        at = t * SLOT
        tail = jnp.where(row16 == 2, pieces(small[t][0:1, :]), acc[at + TOK : at + SLOT])
        if t == 0:
            own_out[0:TOK] = acc[0:TOK]
            own_out[TOK:SLOT] = tail
        else:
            sends[t - 1][0:TOK] = acc[at : at + TOK].astype(BF16)
            sends[t - 1][TOK:SLOT] = tail.astype(BF16)


def build_kernel(place, mods, *refs):
    build(place, mods, refs[0:8], refs[8], refs[9])


def key_kernel(h_ref, small, *refs):
    multiply(h_ref, small, lambda ring: refs[ring][...], refs[4], refs[5:8])


def value_query_kernel(h_ref, *refs):
    weights, own_out, sends = refs[0:4], refs[4], refs[5:8]
    for part in range(2):
        cols = slice(part * W, (part + 1) * W)
        acc = dot(h_ref[0], weights[0][cols, :])
        for ring in range(1, 4):
            acc = acc + dot(h_ref[ring], weights[ring][cols, :])
        own_out[:, cols] = acc[0:SLOT]
        for t in range(1, 4):
            sends[t - 1][:, cols] = acc[t * SLOT : (t + 1) * SLOT].astype(BF16)


def key_sum_kernel(own, a, b, c, key_out, norm_out):
    tail = own[TOK:, 0:W] + a[TOK:, 0:W].astype(F32) + b[TOK:, 0:W].astype(F32) + c[TOK:, 0:W].astype(F32)
    r = lax.rsqrt(joined(tail[2:3, :]) * (1.0 / (16 * W)) + 1e-06)
    norm = jnp.broadcast_to(r, (TOK, 128)).T
    norm_out[...] = norm
    tops = jnp.zeros((1, HD), F32)
    for head in range(3):
        cols = slice(head * HD, (head + 1) * HD)
        k = own[0:TOK, cols] + a[0:TOK, cols].astype(F32) + b[0:TOK, cols].astype(F32) + c[0:TOK, cols].astype(F32)
        k = k * norm + (tail[0:1, cols] + tail[1:2, cols])
        key_out[0:TOK, cols] = k.astype(BF16)
        tops = jnp.maximum(tops, jnp.max(jnp.abs(k), axis=0, keepdims=True))
    key_out[TOK:] = jnp.broadcast_to(pieces(tops), (16, W)).astype(BF16)


def summed(own, a, b, c, norm, first):
    out = []
    for head in range(3):
        cols = slice(first + head * HD, first + (head + 1) * HD)
        total = own[:, cols] + a[:, cols].astype(F32) + b[:, cols].astype(F32) + c[:, cols].astype(F32)
        out.append(total[0:TOK] * norm + (total[TOK : TOK + 1] + total[TOK + 1 : TOK + 2]))
    return out


def value_sum_kernel(first, own, a, b, c, norm, out):
    for head, v in enumerate(summed(own, a, b, c, norm[...], first)):
        out[:, head * HD : (head + 1) * HD] = v.astype(BF16)


def largest(tails):
    tops = [joined(t[TOK:, :].astype(F32)[0:1, :]) for t in tails]
    return jnp.maximum(jnp.maximum(tops[0], tops[1]), jnp.maximum(tops[2], tops[3]))


def top_kernel(t0, t1, t2, t3, out):
    out[...] = jnp.broadcast_to(largest([t0, t1, t2, t3]), (8, HD))


def query_sum_kernel(first, own, a, b, c, norm, amax, out):
    for head, q in enumerate(summed(own, a, b, c, norm[...], first)):
        out[0:TOK, head * HD : (head + 1) * HD] = q.astype(BF16)
    out[TOK:] = jnp.broadcast_to(pieces(amax[0:1, :]), (16, W)).astype(BF16)


def attend_kernel(limits, *refs):
    queries, keys, values, outs = refs[0:4], refs[4:8], refs[8:12], refs[12:16]
    factor = KEY_BOUND / (largest(queries) + 1e-06) * HD ** (-0.5)
    column = lax.broadcasted_iota(jnp.int32, (1, 4 * TOK), 1)
    inner = column % TOK
    col128 = lax.broadcasted_iota(jnp.int32, (TOK, 128), 1)
    masks = []
    for t in range(4):
        limit = jnp.zeros((1, 4 * TOK), jnp.int32)
        for u in range(4):
            limit = jnp.where(column // TOK == u, limits[t * 4 + u], limit)
        masks.append(inner < limit)
    stats = [jnp.zeros((TOK, 128), F32) for _ in range(4)]
    for head in range(3):
        cols = slice(head * HD, (head + 1) * HD)
        k = jnp.concatenate([ref[0:TOK, cols] for ref in keys], axis=0)
        v = jnp.concatenate([ref[:, cols] for ref in values], axis=0)
        for t in range(4):
            allowed = jnp.broadcast_to(masks[t], (TOK, 4 * TOK))
            q = (queries[t][0:TOK, cols].astype(F32) * factor).astype(BF16)
            s = lax.dot_general(q, k, (((1,), (1,)), ((), ())), preferred_element_type=F32)
            s = jnp.where(allowed, s, NEG)
            top = jnp.max(s, axis=1, keepdims=True)
            w = jnp.where(allowed, jnp.exp(s - top), 0.0)
            total = jnp.sum(w, axis=1, keepdims=True)
            some = total > 0.0
            safe = jnp.where(some, total, 1.0)
            outs[t][:, cols] = (dot(w.astype(BF16), v) / safe).astype(BF16)
            lse = jnp.where(some, top + jnp.log(safe), NEG)
            for piece in range(3):
                part = rounded(lse)
                stats[t] = jnp.where(col128 == head * 3 + piece, part, stats[t])
                lse = lse - part
    for t in range(4):
        outs[t][:, W:] = stats[t].astype(BF16)


def merge_kernel(*refs):
    parts, out = refs[0:4], refs[4]
    stats = [p[:, W:].astype(F32) for p in parts]
    for head in range(3):
        cols = slice(head * HD, (head + 1) * HD)
        at = head * 3
        lse = [s[:, at : at + 1] + s[:, at + 1 : at + 2] + s[:, at + 2 : at + 3] for s in stats]
        top = jnp.maximum(jnp.maximum(lse[0], lse[1]), jnp.maximum(lse[2], lse[3]))
        share = [jnp.exp(e - top) for e in lse]
        acc = share[0] * parts[0][:, cols].astype(F32)
        for i in range(1, 4):
            acc = acc + share[i] * parts[i][:, cols].astype(F32)
        out[:, cols] = (acc / (share[0] + share[1] + share[2] + share[3])).astype(BF16)


def project_kernel(place, *refs):
    attended, weights, out, o_all, w_all = refs[0:4], refs[4:8], refs[8], refs[9], refs[10]
    turn, zl, parity = place[0], place[1], place[2]
    for t in range(4):
        o_all[t] = attended[t][...]
        w_all[t] = weights[t][...]
    rows = jnp.concatenate([o_all[(turn + s) & 3] for s in range(4)], axis=0)
    for half in range(2):
        ring = (zl - (2 * half + parity)) & 3
        out[:, half * W : (half + 1) * W] = dot(rows, w_all[ring]).astype(BF16)


def project(place, attended, weights):
    return call(
        project_kernel,
        [((4 * TOK, 2 * W), BF16)],
        scratch=[pltpu.VMEM((4, TOK, W), BF16), pltpu.VMEM((4, W, W), BF16)],
        smem=1,
        n_in=8,
        room=10,
    )(place, *attended, *weights)[0]


def core_sum_kernel(a, b, own, *sends):
    own[...] = a[0:TOK].astype(F32) + b[0:TOK].astype(F32)
    for s in range(1, 4):
        rows = slice(s * TOK, (s + 1) * TOK)
        sends[s - 1][...] = (a[rows].astype(F32) + b[rows].astype(F32)).astype(BF16)


def y_sum_kernel(own, a, b, c, gate, keep, base, out):
    total = own[...] + a[...].astype(F32) + b[...].astype(F32) + c[...].astype(F32)
    out[...] = (total * gate[...] + base[...].astype(F32) * keep[...]).astype(BF16)


def after(a, dep):
    return lax.optimization_barrier((a, dep))[0]


def pick(flag, a, b):
    return jnp.where(flag, a, b)


def on_device(hidden, fresh, w_qkv, w_out, mod_table, levels, block_mask, counts):
    ctx_at = lax.axis_index("ctx")
    head_at = lax.axis_index("head")
    x, zl = ctx_at // 4, ctx_at % 4
    y, zh, core = head_at // 4, (head_at // 2) % 2, head_at % 2
    four = jnp.arange(4, dtype=jnp.int32)
    ids = jnp.arange(BLOCKS, dtype=jnp.int32)

    a0, a1 = turned(hidden, 0), turned(hidden, 1)
    pair = pick(zh == 0, jnp.concatenate([a0, a1], 1), jnp.concatenate([a1, a0], 1))

    w_k = [w_qkv[1], zl_shift(w_qkv[1], 1), zl_shift(w_qkv[1], 3)]
    w_vq = jnp.concatenate([w_qkv[2], w_qkv[0]], 0)

    chunks = [(x * 4 + 2 * half + c) * W for c in (core, 1 - core) for half in (0, 1)]
    mod_chunks = [lax.dynamic_slice_in_dim(mod_table, at, W, 2) for at in chunks]
    mod_own = jnp.concatenate(mod_chunks[:2], 2)
    mod_other = jnp.concatenate(mod_chunks[2:], 2)
    level_ids = jnp.arange(mod_table.shape[1], dtype=jnp.int32)

    def rows_at(table, level):
        hot = level[..., None] == level_ids
        return jnp.sum(jnp.where(hot[..., None], table, 0.0), axis=-2)

    def level_of(step, blocks):
        return jnp.sum(jnp.where(blocks[..., None] == ids, levels[step], 0), axis=-1)

    slot_blocks = (y - four) % 4 * 4 + zl
    dest_block = y * 4 + zl
    fresh_pair = jnp.concatenate([lax.dynamic_slice_in_dim(fresh, at, W, 1) for at in chunks[:2]], 1)

    key_place = jnp.stack([(y - x) % 4, zl, core]).astype(jnp.int32)
    keep_place = jnp.stack([(x - y) % 4, zl, core]).astype(jnp.int32)
    send_place = jnp.stack([(x - y) % 4, zl, 1 - core]).astype(jnp.int32)
    query_blocks = (x - four) % 4 * 4 + zl
    key_blocks = x * 4 + (zl - four) % 4
    def small_for(step):
        slots, queried, keyed, here = ((b - step) % BLOCKS for b in (slot_blocks, query_blocks, key_blocks, dest_block))
        lv = level_of(step, slots)
        mods = jnp.concatenate([rows_at(m[k], lv) for m in (mod_own, mod_other) for k in (1, 0)], 0)
        seen = jnp.sum(jnp.where((queried[:, None] == ids)[..., None], block_mask, 0), axis=1)
        seen = jnp.sum(jnp.where(keyed[:, None] == ids, seen[:, None, :], 0), axis=-1)
        live = jnp.sum(jnp.where(keyed[:, None] == ids, counts[step : step + BLOCKS], 0), axis=-1)
        gate = rows_at(mod_own[2], level_of(step, here))[None]
        half = jnp.arange(2 * W, dtype=jnp.int32)[None] // W
        keep = jnp.where(zh == (half if step else 0), 1.0, 0.0) + jnp.zeros((1, 2 * W), F32)
        return mods, (seen * live).reshape(16).astype(jnp.int32), gate, keep

    smalls = [small_for(step) for step in range(2)]
    pair, w_k, smalls, fresh_pair = lax.optimization_barrier((pair, w_k, smalls, fresh_pair))
    w_k.insert(2, zl_shift(w_k[1], 1))
    w_vq = after(w_vq, w_k[2])
    w_vq = [w_vq, zl_shift(w_vq, 1), zl_shift(w_vq, 3)]
    w_o = [w_out]

    def forward(ring, dep):
        ring.insert(2, zl_shift(after(ring[1], dep), 1))

    def layer(pair, step):
        mods, limits, gate, keep = smalls[step]
        own = [pair] + [y_shift(pair, s) for s in (1, 2, 3)]
        other = [core_swap(a) for a in own]
        h, small = call(build_kernel, [((4, 4 * SLOT, W), BF16), ((4, 8, 128), F32)], smem=1, n_in=9, room=10)(
            key_place, mods, *own, *other
        )
        key_types = [((SLOT, W), F32)] + [((SLOT, W), BF16)] * 3
        k_own, *k_sends = call(key_kernel, key_types, n_in=6, room=10)(h, small, *w_k)
        k_got = [x_shift(k_sends[t - 1], t) for t in (1, 2, 3)]
        k_c, norm = call(key_sum_kernel, [((SLOT, W), BF16), ((TOK, 128), F32)], n_in=4)(k_own, *k_got)
        keys = [k_c] + [zl_shift(k_c, u) for u in (1, 2, 3)]
        if step == 0:
            forward(w_vq, keys)
        amax = call(top_kernel, [((8, HD), F32)], n_in=4)(*keys)[0]
        amax = jnp.maximum(amax, head_swap(amax, 1))
        amax = jnp.maximum(amax, head_swap(amax, 2))
        near = amax
        amax = jnp.maximum(amax, head_swap(amax, 4))
        amax = jnp.maximum(amax, head_swap(amax, 8))
        vq_own, *vq_sends = call(
            value_query_kernel,
            [((SLOT, 2 * W), F32)] + [((SLOT, 2 * W), BF16)] * 3,
            n_in=5,
            room=16,
        )(after(h, near) if step == 0 else h, *w_vq)
        if step == 1:
            *vq_sends, _ = lax.optimization_barrier((*vq_sends, keys[1]))
        vq_got = [x_shift(vq_sends[t - 1], t) for t in (1, 2, 3)]
        v_c = call(functools.partial(value_sum_kernel, 0), [((TOK, W), BF16)], n_in=5)(vq_own, *vq_got, norm)[0]
        v_c = after(v_c, near)
        values = [v_c] + [zl_shift(v_c, u) for u in (1, 2, 3)]
        q_b = call(functools.partial(query_sum_kernel, W), [((SLOT, W), BF16)], n_in=6)(
            vq_own, *vq_got, norm, amax
        )[0]
        queries = [q_b] + [x_shift(q_b, t) for t in (1, 2, 3)]
        if step == 0:
            start = after(w_out, queries[1])
            w_o.extend([zl_shift(start, 1), zl_shift(start, 3)])
        parts = call(attend_kernel, [((TOK, W + 128), BF16)] * 4, smem=1, n_in=12, room=12)(
            limits, *queries, *keys, *values
        )
        got = [x_shift(parts[t], -t) for t in (1, 2, 3)]
        o = call(merge_kernel, [((TOK, W), BF16)], n_in=4)(parts[0], *got)[0]
        if step == 0:
            forward(w_o, parts[0])
        attended = [o] + [x_shift(o, t) for t in (1, 2, 3)]
        sent = core_swap(project(send_place, attended, w_o))
        kept = project(keep_place, attended, w_o)
        own_sum, *sends = call(
            core_sum_kernel, [((TOK, 2 * W), F32)] + [((TOK, 2 * W), BF16)] * 3, n_in=2
        )(kept, sent)
        got = [y_shift(sends[s - 1], -s) for s in (1, 2, 3)]
        return call(y_sum_kernel, [((TOK, 2 * W), BF16)], n_in=7)(own_sum, *got, gate, keep, pair)[0]

    share = layer(pair, 0)
    first = (share.astype(F32) + head_swap(share, 2).astype(F32)).astype(BF16)
    second = pick(dest_block == 0, fresh_pair, first)
    share = layer(second, 1)
    mine_half = pick(zh == 0, share[:, :W], share[:, W:])
    other_half = pick(zh == 0, share[:, W:], share[:, :W])
    return (turned(mine_half, 0, 1).astype(F32) + turned(other_half, 1, 1).astype(F32)).astype(BF16)


def solution(mesh):
    return jax.shard_map(
        on_device,
        mesh=mesh,
        in_specs=(
            P("ctx", "head"),
            P(),
            P(None, "ctx", "head"),
            P("head", "ctx"),
            P(),
            P(),
            P(),
            P(),
        ),
        out_specs=P("ctx", "head"),
        check_vma=False,
    )
```

```python
import functools

import jax
import jax.numpy as jnp
from jax import lax
from jax.experimental import pallas as pl
from jax.experimental.pallas import tpu as pltpu
from jax.sharding import PartitionSpec as P

HD = 128
TOK = 128
W = 384
BLOCKS = 16
KEY_BOUND = 8.0
NEG = -1e30
F32 = jnp.float32
BF16 = jnp.bfloat16

BOTH = ("ctx", "head")


def coords():
    return [(x, zl, y, zh, core) for x in range(4) for zl in range(4) for y in range(4) for zh in range(2) for core in range(2)]


def flat(x, zl, y, zh, core):
    return ((x * 4 + zl) * 4 + y) * 4 + zh * 2 + core


def x_shift(a, t):
    return lax.ppermute(a, "ctx", [(c, (c + 4 * t) % 16) for c in range(16)])


def zl_shift(a, t):
    return lax.ppermute(a, "ctx", [(c, c // 4 * 4 + (c + t) % 4) for c in range(16)])


def y_shift(a, t):
    return lax.ppermute(a, "head", [(g, (g + 4 * t) % 16) for g in range(16)])


def head_swap(a, bit):
    return lax.ppermute(a, "head", [(g, g ^ bit) for g in range(16)])


def core_swap(a):
    return head_swap(a, 1)


def turned(a, flip, back=0):
    pairs = []
    for x, zl, y, zh, core in coords():
        to_x, to_zl = divmod((y * 4 + zl - back) % BLOCKS, 4)
        pairs.append((flat(x, zl, y, zh, core), flat(to_x, to_zl, x, zh ^ flip, core)))
    return lax.ppermute(a, BOTH, pairs)


def call(kernel, outs, scratch=(), smem=0, n_in=0, n_far=0, room=6):
    specs = [pl.BlockSpec(memory_space=pltpu.SMEM)] * smem + [pl.BlockSpec(memory_space=pltpu.VMEM)] * n_in
    specs += [pl.BlockSpec(memory_space=pltpu.HBM)] * n_far
    return pl.pallas_call(
        kernel,
        out_shape=[jax.ShapeDtypeStruct(s, d) for s, d in outs],
        in_specs=specs,
        out_specs=[pl.BlockSpec(memory_space=pltpu.VMEM)] * len(outs),
        scratch_shapes=list(scratch),
        compiler_params=pltpu.CompilerParams(vmem_limit_bytes=room * 1024 * 1024),
    )


def dot(a, b):
    return jnp.dot(a, b, preferred_element_type=F32)


def rounded(a):
    return a.astype(BF16).astype(F32)


def pieces(row):
    high = rounded(row)
    middle = rounded(row - high)
    return jnp.concatenate([high, middle, row - high - middle], axis=1)


def joined(row):
    return row[:, 0:HD] + row[:, HD : 2 * HD] + row[:, 2 * HD : 3 * HD]


SLOT = TOK + 16


def build(place, mods, tiles, h_ref, small):
    turn, zl, core = place[0], place[1], place[2]
    row16 = lax.broadcasted_iota(jnp.int32, (16, W), 0)
    column = lax.broadcasted_iota(jnp.int32, (TOK, 128), 1)
    table = jnp.zeros((TOK, 128), F32)
    for s in range(4):
        start = ((turn - s) & 3) * SLOT
        rows = pl.ds(pl.multiple_of(start, 16), TOK)
        extra = pl.ds(pl.multiple_of(start + TOK, 16), 16)
        total = jnp.zeros((TOK, 1), F32)
        for tile_ref, at, c in ((tiles[s], s, core), (tiles[4 + s], 8 + s, 1 - core)):
            scale, shift = mods[at : at + 1, :], mods[at + 4 : at + 5, :]
            tile = tile_ref[...].astype(F32)
            total = total + jnp.sum(tile * tile, axis=1, keepdims=True)
            scaled = (tile * (1.0 + scale)).astype(BF16)
            for half in range(2):
                cols = slice(half * W, (half + 1) * W)
                ring = (zl - (2 * half + c)) & 3
                high = rounded(shift[:, cols])
                low = shift[:, cols] - high
                h_ref[ring, rows, :] = scaled[:, cols]
                h_ref[ring, extra, :] = jnp.where(row16 == 0, high, jnp.where(row16 == 1, low, 0.0)).astype(BF16)
        table = jnp.where(column == s, total, table)
    table = table.T
    for s in range(4):
        small[(turn - s) & 3] = jnp.broadcast_to(table[s : s + 1, :], (8, 128))


def multiply(h_ref, small, weight, own_out, sends):
    row16 = lax.broadcasted_iota(jnp.int32, (16, W), 0)
    acc = None
    for ring in range(4):
        term = dot(h_ref[ring], weight(ring))
        acc = term if acc is None else acc + term
    for t in range(4):
        at = t * SLOT
        tail = jnp.where(row16 == 2, pieces(small[t][0:1, :]), acc[at + TOK : at + SLOT])
        if t == 0:
            own_out[0:TOK] = acc[0:TOK]
            own_out[TOK:SLOT] = tail
        else:
            sends[t - 1][0:TOK] = acc[at : at + TOK].astype(BF16)
            sends[t - 1][TOK:SLOT] = tail.astype(BF16)


def build_kernel(place, mods, *refs):
    build(place, mods, refs[0:8], refs[8], refs[9])


def key_kernel(h_ref, small, *refs):
    multiply(h_ref, small, lambda ring: refs[ring][...], refs[4], refs[5:8])


def value_query_kernel(h_ref, *refs):
    weights, own_out, sends = refs[0:4], refs[4], refs[5:8]
    for part in range(2):
        cols = slice(part * W, (part + 1) * W)
        acc = dot(h_ref[0], weights[0][cols, :])
        for ring in range(1, 4):
            acc = acc + dot(h_ref[ring], weights[ring][cols, :])
        own_out[:, cols] = acc[0:SLOT]
        for t in range(1, 4):
            sends[t - 1][:, cols] = acc[t * SLOT : (t + 1) * SLOT].astype(BF16)


def key_sum_kernel(own, a, b, c, key_out, norm_out):
    tail = own[TOK:, 0:W] + a[TOK:, 0:W].astype(F32) + b[TOK:, 0:W].astype(F32) + c[TOK:, 0:W].astype(F32)
    r = lax.rsqrt(joined(tail[2:3, :]) * (1.0 / (16 * W)) + 1e-06)
    norm = jnp.broadcast_to(r, (TOK, 128)).T
    norm_out[...] = norm
    tops = jnp.zeros((1, HD), F32)
    for head in range(3):
        cols = slice(head * HD, (head + 1) * HD)
        k = own[0:TOK, cols] + a[0:TOK, cols].astype(F32) + b[0:TOK, cols].astype(F32) + c[0:TOK, cols].astype(F32)
        k = k * norm + (tail[0:1, cols] + tail[1:2, cols])
        key_out[0:TOK, cols] = k.astype(BF16)
        tops = jnp.maximum(tops, jnp.max(jnp.abs(k), axis=0, keepdims=True))
    key_out[TOK:] = jnp.broadcast_to(pieces(tops), (16, W)).astype(BF16)


def summed(own, a, b, c, norm, first):
    out = []
    for head in range(3):
        cols = slice(first + head * HD, first + (head + 1) * HD)
        total = own[:, cols] + a[:, cols].astype(F32) + b[:, cols].astype(F32) + c[:, cols].astype(F32)
        out.append(total[0:TOK] * norm + (total[TOK : TOK + 1] + total[TOK + 1 : TOK + 2]))
    return out


def value_sum_kernel(first, own, a, b, c, norm, out):
    for head, v in enumerate(summed(own, a, b, c, norm[...], first)):
        out[:, head * HD : (head + 1) * HD] = v.astype(BF16)


def largest(tails):
    tops = [joined(t[TOK:, :].astype(F32)[0:1, :]) for t in tails]
    return jnp.maximum(jnp.maximum(tops[0], tops[1]), jnp.maximum(tops[2], tops[3]))


def top_kernel(t0, t1, t2, t3, out):
    out[...] = jnp.broadcast_to(largest([t0, t1, t2, t3]), (8, HD))


def query_sum_kernel(first, own, a, b, c, norm, amax, out):
    for head, q in enumerate(summed(own, a, b, c, norm[...], first)):
        out[0:TOK, head * HD : (head + 1) * HD] = q.astype(BF16)
    out[TOK:] = jnp.broadcast_to(pieces(amax[0:1, :]), (16, W)).astype(BF16)


def attend_kernel(limits, *refs):
    queries, keys, values, outs = refs[0:4], refs[4:8], refs[8:12], refs[12:16]
    factor = KEY_BOUND / (largest(queries) + 1e-06) * HD ** (-0.5)
    column = lax.broadcasted_iota(jnp.int32, (1, 4 * TOK), 1)
    inner = column % TOK
    col128 = lax.broadcasted_iota(jnp.int32, (TOK, 128), 1)
    masks = []
    for t in range(4):
        limit = jnp.zeros((1, 4 * TOK), jnp.int32)
        for u in range(4):
            limit = jnp.where(column // TOK == u, limits[t * 4 + u], limit)
        masks.append(inner < limit)
    stats = [jnp.zeros((TOK, 128), F32) for _ in range(4)]
    for head in range(3):
        cols = slice(head * HD, (head + 1) * HD)
        k = jnp.concatenate([ref[0:TOK, cols] for ref in keys], axis=0)
        v = jnp.concatenate([ref[:, cols] for ref in values], axis=0)
        for t in range(4):
            allowed = jnp.broadcast_to(masks[t], (TOK, 4 * TOK))
            q = (queries[t][0:TOK, cols].astype(F32) * factor).astype(BF16)
            s = lax.dot_general(q, k, (((1,), (1,)), ((), ())), preferred_element_type=F32)
            s = jnp.where(allowed, s, NEG)
            top = jnp.max(s, axis=1, keepdims=True)
            w = jnp.where(allowed, jnp.exp(s - top), 0.0)
            total = jnp.sum(w, axis=1, keepdims=True)
            some = total > 0.0
            safe = jnp.where(some, total, 1.0)
            outs[t][:, cols] = (dot(w.astype(BF16), v) / safe).astype(BF16)
            lse = jnp.where(some, top + jnp.log(safe), NEG)
            for piece in range(3):
                part = rounded(lse)
                stats[t] = jnp.where(col128 == head * 3 + piece, part, stats[t])
                lse = lse - part
    for t in range(4):
        outs[t][:, W:] = stats[t].astype(BF16)


def merge_kernel(*refs):
    parts, out = refs[0:4], refs[4]
    stats = [p[:, W:].astype(F32) for p in parts]
    for head in range(3):
        cols = slice(head * HD, (head + 1) * HD)
        at = head * 3
        lse = [s[:, at : at + 1] + s[:, at + 1 : at + 2] + s[:, at + 2 : at + 3] for s in stats]
        top = jnp.maximum(jnp.maximum(lse[0], lse[1]), jnp.maximum(lse[2], lse[3]))
        share = [jnp.exp(e - top) for e in lse]
        acc = share[0] * parts[0][:, cols].astype(F32)
        for i in range(1, 4):
            acc = acc + share[i] * parts[i][:, cols].astype(F32)
        out[:, cols] = (acc / (share[0] + share[1] + share[2] + share[3])).astype(BF16)


def project_kernel(place, *refs):
    attended, weights, out, o_all, w_all = refs[0:4], refs[4:8], refs[8], refs[9], refs[10]
    turn, zl, parity = place[0], place[1], place[2]
    for t in range(4):
        o_all[t] = attended[t][...]
        w_all[t] = weights[t][...]
    rows = jnp.concatenate([o_all[(turn + s) & 3] for s in range(4)], axis=0)
    for half in range(2):
        ring = (zl - (2 * half + parity)) & 3
        out[:, half * W : (half + 1) * W] = dot(rows, w_all[ring]).astype(BF16)


def project(place, attended, weights):
    return call(
        project_kernel,
        [((4 * TOK, 2 * W), BF16)],
        scratch=[pltpu.VMEM((4, TOK, W), BF16), pltpu.VMEM((4, W, W), BF16)],
        smem=1,
        n_in=8,
        room=10,
    )(place, *attended, *weights)[0]


def core_sum_kernel(a, b, own, *sends):
    own[...] = a[0:TOK].astype(F32) + b[0:TOK].astype(F32)
    for s in range(1, 4):
        rows = slice(s * TOK, (s + 1) * TOK)
        sends[s - 1][...] = (a[rows].astype(F32) + b[rows].astype(F32)).astype(BF16)


def y_sum_kernel(own, a, b, c, gate, keep, base, out):
    total = own[...] + a[...].astype(F32) + b[...].astype(F32) + c[...].astype(F32)
    out[...] = (total * gate[...] + base[...].astype(F32) * keep[...]).astype(BF16)


def after(a, dep):
    return lax.optimization_barrier((a, dep))[0]


def pick(flag, a, b):
    return jnp.where(flag, a, b)


def on_device(hidden, fresh, w_qkv, w_out, mod_table, levels, block_mask, counts):
    ctx_at = lax.axis_index("ctx")
    head_at = lax.axis_index("head")
    x, zl = ctx_at // 4, ctx_at % 4
    y, zh, core = head_at // 4, (head_at // 2) % 2, head_at % 2
    four = jnp.arange(4, dtype=jnp.int32)
    ids = jnp.arange(BLOCKS, dtype=jnp.int32)

    a0, a1 = turned(hidden, 0), turned(hidden, 1)
    pair = pick(zh == 0, jnp.concatenate([a0, a1], 1), jnp.concatenate([a1, a0], 1))

    w_k = [w_qkv[1], zl_shift(w_qkv[1], 1), zl_shift(w_qkv[1], 3)]
    w_vq = jnp.concatenate([w_qkv[2], w_qkv[0]], 0)

    chunks = [(x * 4 + 2 * half + c) * W for c in (core, 1 - core) for half in (0, 1)]
    mod_chunks = [lax.dynamic_slice_in_dim(mod_table, at, W, 2) for at in chunks]
    mod_own = jnp.concatenate(mod_chunks[:2], 2)
    mod_other = jnp.concatenate(mod_chunks[2:], 2)
    level_ids = jnp.arange(mod_table.shape[1], dtype=jnp.int32)

    def rows_at(table, level):
        hot = level[..., None] == level_ids
        return jnp.sum(jnp.where(hot[..., None], table, 0.0), axis=-2)

    def level_of(step, blocks):
        return jnp.sum(jnp.where(blocks[..., None] == ids, levels[step], 0), axis=-1)

    slot_blocks = (y - four) % 4 * 4 + zl
    dest_block = y * 4 + zl
    fresh_pair = jnp.concatenate([lax.dynamic_slice_in_dim(fresh, at, W, 1) for at in chunks[:2]], 1)

    key_place = jnp.stack([(y - x) % 4, zl, core]).astype(jnp.int32)
    keep_place = jnp.stack([(x - y) % 4, zl, core]).astype(jnp.int32)
    send_place = jnp.stack([(x - y) % 4, zl, 1 - core]).astype(jnp.int32)
    query_blocks = (x - four) % 4 * 4 + zl
    key_blocks = x * 4 + (zl - four) % 4
    def small_for(step):
        slots, queried, keyed, here = ((b - step) % BLOCKS for b in (slot_blocks, query_blocks, key_blocks, dest_block))
        lv = level_of(step, slots)
        mods = jnp.concatenate([rows_at(m[k], lv) for m in (mod_own, mod_other) for k in (1, 0)], 0)
        seen = jnp.sum(jnp.where((queried[:, None] == ids)[..., None], block_mask, 0), axis=1)
        seen = jnp.sum(jnp.where(keyed[:, None] == ids, seen[:, None, :], 0), axis=-1)
        live = jnp.sum(jnp.where(keyed[:, None] == ids, counts[step : step + BLOCKS], 0), axis=-1)
        gate = rows_at(mod_own[2], level_of(step, here))[None]
        half = jnp.arange(2 * W, dtype=jnp.int32)[None] // W
        keep = jnp.where(zh == (half if step else 0), 1.0, 0.0) + jnp.zeros((1, 2 * W), F32)
        return mods, (seen * live).reshape(16).astype(jnp.int32), gate, keep

    smalls = [small_for(step) for step in range(2)]
    pair, w_k, smalls, fresh_pair = lax.optimization_barrier((pair, w_k, smalls, fresh_pair))
    w_k.insert(2, zl_shift(w_k[1], 1))
    w_vq = [w_vq]
    w_o = [w_out]

    def forward(ring, dep):
        ring.insert(2, zl_shift(after(ring[1], dep), 1))

    def layer(pair, step):
        mods, limits, gate, keep = smalls[step]
        own = [pair] + [y_shift(pair, s) for s in (1, 2, 3)]
        if step == 0:
            w_vq.append(zl_shift(after(w_vq[0], own[1]), 1))
        other = [core_swap(a) for a in own]
        h, small = call(build_kernel, [((4, 4 * SLOT, W), BF16), ((4, 8, 128), F32)], smem=1, n_in=9, room=10)(
            key_place, mods, *own, *other
        )
        key_types = [((SLOT, W), F32)] + [((SLOT, W), BF16)] * 3
        k_own, *k_sends = call(key_kernel, key_types, n_in=6, room=10)(h, small, *w_k)
        k_got = [x_shift(k_sends[t - 1], t) for t in (1, 2, 3)]
        k_c, norm = call(key_sum_kernel, [((SLOT, W), BF16), ((TOK, 128), F32)], n_in=4)(k_own, *k_got)
        keys = [k_c] + [zl_shift(k_c, u) for u in (1, 2, 3)]
        if step == 0:
            w_vq.append(zl_shift(after(w_vq[1], k_c), 1))
        amax = call(top_kernel, [((8, HD), F32)], n_in=4)(*keys)[0]
        amax = jnp.maximum(amax, head_swap(amax, 1))
        amax = jnp.maximum(amax, head_swap(amax, 2))
        near = amax
        if step == 0:
            w_vq.append(zl_shift(after(w_vq[2], near), 1))
        amax = jnp.maximum(amax, head_swap(amax, 4))
        amax = jnp.maximum(amax, head_swap(amax, 8))
        vq_own, *vq_sends = call(
            value_query_kernel,
            [((SLOT, 2 * W), F32)] + [((SLOT, 2 * W), BF16)] * 3,
            n_in=5,
            room=16,
        )(after(h, amax) if step == 0 else h, *w_vq)
        if step == 1:
            *vq_sends, _ = lax.optimization_barrier((*vq_sends, keys))
        vq_got = [x_shift(vq_sends[t - 1], t) for t in (1, 2, 3)]
        v_c = call(functools.partial(value_sum_kernel, 0), [((TOK, W), BF16)], n_in=5)(vq_own, *vq_got, norm)[0]
        v_c = after(v_c, near)
        values = [v_c] + [zl_shift(v_c, u) for u in (1, 2, 3)]
        q_b = call(functools.partial(query_sum_kernel, W), [((SLOT, W), BF16)], n_in=6)(
            vq_own, *vq_got, norm, amax
        )[0]
        queries = [q_b] + [x_shift(q_b, t) for t in (1, 2, 3)]
        if step == 0:
            start = after(w_out, queries[1])
            w_o.extend([zl_shift(start, 1), zl_shift(start, 3)])
        parts = call(attend_kernel, [((TOK, W + 128), BF16)] * 4, smem=1, n_in=12, room=12)(
            limits, *queries, *keys, *values
        )
        got = [x_shift(parts[t], -t) for t in (1, 2, 3)]
        o = call(merge_kernel, [((TOK, W), BF16)], n_in=4)(parts[0], *got)[0]
        if step == 0:
            forward(w_o, parts[0])
        attended = [o] + [x_shift(o, t) for t in (1, 2, 3)]
        sent = core_swap(project(send_place, attended, w_o))
        kept = project(keep_place, attended, w_o)
        own_sum, *sends = call(
            core_sum_kernel, [((TOK, 2 * W), F32)] + [((TOK, 2 * W), BF16)] * 3, n_in=2
        )(kept, sent)
        got = [y_shift(sends[s - 1], -s) for s in (1, 2, 3)]
        return call(y_sum_kernel, [((TOK, 2 * W), BF16)], n_in=7)(own_sum, *got, gate, keep, pair)[0]

    share = layer(pair, 0)
    first = (share.astype(F32) + head_swap(share, 2).astype(F32)).astype(BF16)
    second = pick(dest_block == 0, fresh_pair, first)
    share = layer(second, 1)
    mine_half = pick(zh == 0, share[:, :W], share[:, W:])
    other_half = pick(zh == 0, share[:, W:], share[:, :W])
    return (turned(mine_half, 0, 1).astype(F32) + turned(other_half, 1, 1).astype(F32)).astype(BF16)


def solution(mesh):
    return jax.shard_map(
        on_device,
        mesh=mesh,
        in_specs=(
            P("ctx", "head"),
            P(),
            P(None, "ctx", "head"),
            P("head", "ctx"),
            P(),
            P(),
            P(),
            P(),
        ),
        out_specs=P("ctx", "head"),
        check_vma=False,
    )
```

```python
import functools

import jax
import jax.numpy as jnp
from jax import lax
from jax.experimental import pallas as pl
from jax.experimental.pallas import tpu as pltpu
from jax.sharding import PartitionSpec as P

HD = 128
TOK = 128
W = 384
BLOCKS = 16
KEY_BOUND = 8.0
NEG = -1e30
F32 = jnp.float32
BF16 = jnp.bfloat16

BOTH = ("ctx", "head")


def coords():
    return [(x, zl, y, zh, core) for x in range(4) for zl in range(4) for y in range(4) for zh in range(2) for core in range(2)]


def flat(x, zl, y, zh, core):
    return ((x * 4 + zl) * 4 + y) * 4 + zh * 2 + core


def x_shift(a, t):
    return lax.ppermute(a, "ctx", [(c, (c + 4 * t) % 16) for c in range(16)])


def zl_shift(a, t):
    return lax.ppermute(a, "ctx", [(c, c // 4 * 4 + (c + t) % 4) for c in range(16)])


def y_shift(a, t):
    return lax.ppermute(a, "head", [(g, (g + 4 * t) % 16) for g in range(16)])


def head_swap(a, bit):
    return lax.ppermute(a, "head", [(g, g ^ bit) for g in range(16)])


def core_swap(a):
    return head_swap(a, 1)


def turned(a, flip, back=0):
    pairs = []
    for x, zl, y, zh, core in coords():
        to_x, to_zl = divmod((y * 4 + zl - back) % BLOCKS, 4)
        pairs.append((flat(x, zl, y, zh, core), flat(to_x, to_zl, x, zh ^ flip, core)))
    return lax.ppermute(a, BOTH, pairs)


def call(kernel, outs, scratch=(), smem=0, n_in=0, n_far=0, room=6):
    specs = [pl.BlockSpec(memory_space=pltpu.SMEM)] * smem + [pl.BlockSpec(memory_space=pltpu.VMEM)] * n_in
    specs += [pl.BlockSpec(memory_space=pltpu.HBM)] * n_far
    return pl.pallas_call(
        kernel,
        out_shape=[jax.ShapeDtypeStruct(s, d) for s, d in outs],
        in_specs=specs,
        out_specs=[pl.BlockSpec(memory_space=pltpu.VMEM)] * len(outs),
        scratch_shapes=list(scratch),
        compiler_params=pltpu.CompilerParams(vmem_limit_bytes=room * 1024 * 1024),
    )


def dot(a, b):
    return jnp.dot(a, b, preferred_element_type=F32)


def rounded(a):
    return a.astype(BF16).astype(F32)


def pieces(row):
    high = rounded(row)
    middle = rounded(row - high)
    return jnp.concatenate([high, middle, row - high - middle], axis=1)


def joined(row):
    return row[:, 0:HD] + row[:, HD : 2 * HD] + row[:, 2 * HD : 3 * HD]


SLOT = TOK + 16


def build(place, mods, tiles, h_ref, small):
    turn, zl, core = place[0], place[1], place[2]
    row16 = lax.broadcasted_iota(jnp.int32, (16, W), 0)
    column = lax.broadcasted_iota(jnp.int32, (TOK, 128), 1)
    table = jnp.zeros((TOK, 128), F32)
    for s in range(4):
        start = ((turn - s) & 3) * SLOT
        rows = pl.ds(pl.multiple_of(start, 16), TOK)
        extra = pl.ds(pl.multiple_of(start + TOK, 16), 16)
        total = jnp.zeros((TOK, 1), F32)
        for tile_ref, at, c in ((tiles[s], s, core), (tiles[4 + s], 8 + s, 1 - core)):
            scale, shift = mods[at : at + 1, :], mods[at + 4 : at + 5, :]
            tile = tile_ref[...].astype(F32)
            total = total + jnp.sum(tile * tile, axis=1, keepdims=True)
            scaled = (tile * (1.0 + scale)).astype(BF16)
            for half in range(2):
                cols = slice(half * W, (half + 1) * W)
                ring = (zl - (2 * half + c)) & 3
                high = rounded(shift[:, cols])
                low = shift[:, cols] - high
                h_ref[ring, rows, :] = scaled[:, cols]
                h_ref[ring, extra, :] = jnp.where(row16 == 0, high, jnp.where(row16 == 1, low, 0.0)).astype(BF16)
        table = jnp.where(column == s, total, table)
    table = table.T
    for s in range(4):
        small[(turn - s) & 3] = jnp.broadcast_to(table[s : s + 1, :], (8, 128))


def multiply(h_ref, small, weight, own_out, sends):
    row16 = lax.broadcasted_iota(jnp.int32, (16, W), 0)
    acc = None
    for ring in range(4):
        term = dot(h_ref[ring], weight(ring))
        acc = term if acc is None else acc + term
    for t in range(4):
        at = t * SLOT
        tail = jnp.where(row16 == 2, pieces(small[t][0:1, :]), acc[at + TOK : at + SLOT])
        if t == 0:
            own_out[0:TOK] = acc[0:TOK]
            own_out[TOK:SLOT] = tail
        else:
            sends[t - 1][0:TOK] = acc[at : at + TOK].astype(BF16)
            sends[t - 1][TOK:SLOT] = tail.astype(BF16)


def build_kernel(place, mods, *refs):
    build(place, mods, refs[0:8], refs[8], refs[9])


def key_kernel(h_ref, small, *refs):
    multiply(h_ref, small, lambda ring: refs[ring][...], refs[4], refs[5:8])


def value_query_kernel(h_ref, *refs):
    weights, own_out, sends = refs[0:4], refs[4], refs[5:8]
    for part in range(2):
        cols = slice(part * W, (part + 1) * W)
        acc = dot(h_ref[0], weights[0][cols, :])
        for ring in range(1, 4):
            acc = acc + dot(h_ref[ring], weights[ring][cols, :])
        own_out[:, cols] = acc[0:SLOT]
        for t in range(1, 4):
            sends[t - 1][:, cols] = acc[t * SLOT : (t + 1) * SLOT].astype(BF16)


def key_sum_kernel(own, a, b, c, key_out, norm_out):
    tail = own[TOK:, 0:W] + a[TOK:, 0:W].astype(F32) + b[TOK:, 0:W].astype(F32) + c[TOK:, 0:W].astype(F32)
    r = lax.rsqrt(joined(tail[2:3, :]) * (1.0 / (16 * W)) + 1e-06)
    norm = jnp.broadcast_to(r, (TOK, 128)).T
    norm_out[...] = norm
    tops = jnp.zeros((1, HD), F32)
    for head in range(3):
        cols = slice(head * HD, (head + 1) * HD)
        k = own[0:TOK, cols] + a[0:TOK, cols].astype(F32) + b[0:TOK, cols].astype(F32) + c[0:TOK, cols].astype(F32)
        k = k * norm + (tail[0:1, cols] + tail[1:2, cols])
        key_out[0:TOK, cols] = k.astype(BF16)
        tops = jnp.maximum(tops, jnp.max(jnp.abs(k), axis=0, keepdims=True))
    key_out[TOK:] = jnp.broadcast_to(pieces(tops), (16, W)).astype(BF16)


def summed(own, a, b, c, norm, first):
    out = []
    for head in range(3):
        cols = slice(first + head * HD, first + (head + 1) * HD)
        total = own[:, cols] + a[:, cols].astype(F32) + b[:, cols].astype(F32) + c[:, cols].astype(F32)
        out.append(total[0:TOK] * norm + (total[TOK : TOK + 1] + total[TOK + 1 : TOK + 2]))
    return out


def value_sum_kernel(first, own, a, b, c, norm, out):
    for head, v in enumerate(summed(own, a, b, c, norm[...], first)):
        out[:, head * HD : (head + 1) * HD] = v.astype(BF16)


def largest(tails):
    tops = [joined(t[TOK:, :].astype(F32)[0:1, :]) for t in tails]
    return jnp.maximum(jnp.maximum(tops[0], tops[1]), jnp.maximum(tops[2], tops[3]))


def top_kernel(t0, t1, t2, t3, out):
    out[...] = jnp.broadcast_to(largest([t0, t1, t2, t3]), (8, HD))


def query_sum_kernel(first, own, a, b, c, norm, amax, out):
    for head, q in enumerate(summed(own, a, b, c, norm[...], first)):
        out[0:TOK, head * HD : (head + 1) * HD] = q.astype(BF16)
    out[TOK:] = jnp.broadcast_to(pieces(amax[0:1, :]), (16, W)).astype(BF16)


def attend_kernel(limits, *refs):
    queries, keys, values, outs = refs[0:4], refs[4:8], refs[8:12], refs[12:16]
    factor = KEY_BOUND / (largest(queries) + 1e-06) * HD ** (-0.5)
    column = lax.broadcasted_iota(jnp.int32, (1, 4 * TOK), 1)
    inner = column % TOK
    col128 = lax.broadcasted_iota(jnp.int32, (TOK, 128), 1)
    masks = []
    for t in range(4):
        limit = jnp.zeros((1, 4 * TOK), jnp.int32)
        for u in range(4):
            limit = jnp.where(column // TOK == u, limits[t * 4 + u], limit)
        masks.append(inner < limit)
    stats = [jnp.zeros((TOK, 128), F32) for _ in range(4)]
    for head in range(3):
        cols = slice(head * HD, (head + 1) * HD)
        k = jnp.concatenate([ref[0:TOK, cols] for ref in keys], axis=0)
        v = jnp.concatenate([ref[:, cols] for ref in values], axis=0)
        for t in range(4):
            allowed = jnp.broadcast_to(masks[t], (TOK, 4 * TOK))
            q = (queries[t][0:TOK, cols].astype(F32) * factor).astype(BF16)
            s = lax.dot_general(q, k, (((1,), (1,)), ((), ())), preferred_element_type=F32)
            s = jnp.where(allowed, s, NEG)
            top = jnp.max(s, axis=1, keepdims=True)
            w = jnp.where(allowed, jnp.exp(s - top), 0.0)
            total = jnp.sum(w, axis=1, keepdims=True)
            some = total > 0.0
            safe = jnp.where(some, total, 1.0)
            outs[t][:, cols] = (dot(w.astype(BF16), v) / safe).astype(BF16)
            lse = jnp.where(some, top + jnp.log(safe), NEG)
            for piece in range(3):
                part = rounded(lse)
                stats[t] = jnp.where(col128 == head * 3 + piece, part, stats[t])
                lse = lse - part
    for t in range(4):
        outs[t][:, W:] = stats[t].astype(BF16)


def merge_kernel(*refs):
    parts, out = refs[0:4], refs[4]
    stats = [p[:, W:].astype(F32) for p in parts]
    for head in range(3):
        cols = slice(head * HD, (head + 1) * HD)
        at = head * 3
        lse = [s[:, at : at + 1] + s[:, at + 1 : at + 2] + s[:, at + 2 : at + 3] for s in stats]
        top = jnp.maximum(jnp.maximum(lse[0], lse[1]), jnp.maximum(lse[2], lse[3]))
        share = [jnp.exp(e - top) for e in lse]
        acc = share[0] * parts[0][:, cols].astype(F32)
        for i in range(1, 4):
            acc = acc + share[i] * parts[i][:, cols].astype(F32)
        out[:, cols] = (acc / (share[0] + share[1] + share[2] + share[3])).astype(BF16)


def project_kernel(place, *refs):
    attended, weights, out, o_all, w_all = refs[0:4], refs[4:8], refs[8], refs[9], refs[10]
    turn, zl, parity = place[0], place[1], place[2]
    for t in range(4):
        o_all[t] = attended[t][...]
        w_all[t] = weights[t][...]
    rows = jnp.concatenate([o_all[(turn + s) & 3] for s in range(4)], axis=0)
    for half in range(2):
        ring = (zl - (2 * half + parity)) & 3
        out[:, half * W : (half + 1) * W] = dot(rows, w_all[ring]).astype(BF16)


def project(place, attended, weights):
    return call(
        project_kernel,
        [((4 * TOK, 2 * W), BF16)],
        scratch=[pltpu.VMEM((4, TOK, W), BF16), pltpu.VMEM((4, W, W), BF16)],
        smem=1,
        n_in=8,
        room=10,
    )(place, *attended, *weights)[0]


def core_sum_kernel(a, b, own, *sends):
    own[...] = a[0:TOK].astype(F32) + b[0:TOK].astype(F32)
    for s in range(1, 4):
        rows = slice(s * TOK, (s + 1) * TOK)
        sends[s - 1][...] = (a[rows].astype(F32) + b[rows].astype(F32)).astype(BF16)


def y_sum_kernel(own, a, b, c, gate, keep, base, out):
    total = own[...] + a[...].astype(F32) + b[...].astype(F32) + c[...].astype(F32)
    out[...] = (total * gate[...] + base[...].astype(F32) * keep[...]).astype(BF16)


def after(a, dep):
    return lax.optimization_barrier((a, dep))[0]


def pick(flag, a, b):
    return jnp.where(flag, a, b)


def on_device(hidden, fresh, w_qkv, w_out, mod_table, levels, block_mask, counts):
    ctx_at = lax.axis_index("ctx")
    head_at = lax.axis_index("head")
    x, zl = ctx_at // 4, ctx_at % 4
    y, zh, core = head_at // 4, (head_at // 2) % 2, head_at % 2
    four = jnp.arange(4, dtype=jnp.int32)
    ids = jnp.arange(BLOCKS, dtype=jnp.int32)

    a0, a1 = turned(hidden, 0), turned(hidden, 1)
    pair = pick(zh == 0, jnp.concatenate([a0, a1], 1), jnp.concatenate([a1, a0], 1))

    w_k = [w_qkv[1], zl_shift(w_qkv[1], 1), zl_shift(w_qkv[1], 3)]
    w_vq = jnp.concatenate([w_qkv[2], w_qkv[0]], 0)

    chunks = [(x * 4 + 2 * half + c) * W for c in (core, 1 - core) for half in (0, 1)]
    mod_chunks = [lax.dynamic_slice_in_dim(mod_table, at, W, 2) for at in chunks]
    mod_own = jnp.concatenate(mod_chunks[:2], 2)
    mod_other = jnp.concatenate(mod_chunks[2:], 2)
    level_ids = jnp.arange(mod_table.shape[1], dtype=jnp.int32)

    def rows_at(table, level):
        hot = level[..., None] == level_ids
        return jnp.sum(jnp.where(hot[..., None], table, 0.0), axis=-2)

    def level_of(step, blocks):
        return jnp.sum(jnp.where(blocks[..., None] == ids, levels[step], 0), axis=-1)

    slot_blocks = (y - four) % 4 * 4 + zl
    dest_block = y * 4 + zl
    fresh_pair = jnp.concatenate([lax.dynamic_slice_in_dim(fresh, at, W, 1) for at in chunks[:2]], 1)

    key_place = jnp.stack([(y - x) % 4, zl, core]).astype(jnp.int32)
    keep_place = jnp.stack([(x - y) % 4, zl, core]).astype(jnp.int32)
    send_place = jnp.stack([(x - y) % 4, zl, 1 - core]).astype(jnp.int32)
    query_blocks = (x - four) % 4 * 4 + zl
    key_blocks = x * 4 + (zl - four) % 4
    def small_for(step):
        slots, queried, keyed, here = ((b - step) % BLOCKS for b in (slot_blocks, query_blocks, key_blocks, dest_block))
        lv = level_of(step, slots)
        mods = jnp.concatenate([rows_at(m[k], lv) for m in (mod_own, mod_other) for k in (1, 0)], 0)
        seen = jnp.sum(jnp.where((queried[:, None] == ids)[..., None], block_mask, 0), axis=1)
        seen = jnp.sum(jnp.where(keyed[:, None] == ids, seen[:, None, :], 0), axis=-1)
        live = jnp.sum(jnp.where(keyed[:, None] == ids, counts[step : step + BLOCKS], 0), axis=-1)
        gate = rows_at(mod_own[2], level_of(step, here))[None]
        half = jnp.arange(2 * W, dtype=jnp.int32)[None] // W
        keep = jnp.where(zh == (half if step else 0), 1.0, 0.0) + jnp.zeros((1, 2 * W), F32)
        return mods, (seen * live).reshape(16).astype(jnp.int32), gate, keep

    smalls = [small_for(step) for step in range(2)]
    pair, w_k, smalls, fresh_pair = lax.optimization_barrier((pair, w_k, smalls, fresh_pair))
    w_k.insert(2, zl_shift(w_k[1], 1))
    w_vq = after(w_vq, w_k[2])
    w_vq = [w_vq, zl_shift(w_vq, 1), zl_shift(w_vq, 3)]
    w_o = [w_out]

    def forward(ring, dep):
        ring.insert(2, zl_shift(after(ring[1], dep), 1))

    def layer(pair, step):
        mods, limits, gate, keep = smalls[step]
        own = [pair] + [y_shift(pair, s) for s in (1, 2, 3)]
        other = [core_swap(a) for a in own]
        h, small = call(build_kernel, [((4, 4 * SLOT, W), BF16), ((4, 8, 128), F32)], smem=1, n_in=9, room=10)(
            key_place, mods, *own, *other
        )
        key_types = [((SLOT, W), F32)] + [((SLOT, W), BF16)] * 3
        k_own, *k_sends = call(key_kernel, key_types, n_in=6, room=10)(h, small, *w_k)
        k_got = [x_shift(k_sends[t - 1], t) for t in (1, 2, 3)]
        k_c, norm = call(key_sum_kernel, [((SLOT, W), BF16), ((TOK, 128), F32)], n_in=4)(k_own, *k_got)
        keys = [k_c] + [zl_shift(k_c, u) for u in (1, 2, 3)]
        if step == 0:
            forward(w_vq, keys)
        arrived = [after(keys[0], w_vq[3])] + keys[1:] if step == 0 else keys
        amax = call(top_kernel, [((8, HD), F32)], n_in=4)(*arrived)[0]
        amax = jnp.maximum(amax, head_swap(amax, 1))
        amax = jnp.maximum(amax, head_swap(amax, 2))
        near = amax
        amax = jnp.maximum(amax, head_swap(amax, 4))
        amax = jnp.maximum(amax, head_swap(amax, 8))
        vq_own, *vq_sends = call(
            value_query_kernel,
            [((SLOT, 2 * W), F32)] + [((SLOT, 2 * W), BF16)] * 3,
            n_in=5,
            room=16,
        )(after(h, near) if step == 0 else h, *w_vq)
        if step == 1:
            *vq_sends, _ = lax.optimization_barrier((*vq_sends, keys[1]))
        vq_got = [x_shift(vq_sends[t - 1], t) for t in (1, 2, 3)]
        v_c = call(functools.partial(value_sum_kernel, 0), [((TOK, W), BF16)], n_in=5)(vq_own, *vq_got, norm)[0]
        v_c = after(v_c, near)
        values = [v_c] + [zl_shift(v_c, u) for u in (1, 2, 3)]
        q_b = call(functools.partial(query_sum_kernel, W), [((SLOT, W), BF16)], n_in=6)(
            vq_own, *vq_got, norm, amax
        )[0]
        queries = [q_b] + [x_shift(q_b, t) for t in (1, 2, 3)]
        if step == 0:
            start = after(w_out, queries[1])
            w_o.extend([zl_shift(start, 1), zl_shift(start, 3)])
        parts = call(attend_kernel, [((TOK, W + 128), BF16)] * 4, smem=1, n_in=12, room=12)(
            limits, *queries, *keys, *values
        )
        got = [x_shift(parts[t], -t) for t in (1, 2, 3)]
        o = call(merge_kernel, [((TOK, W), BF16)], n_in=4)(parts[0], *got)[0]
        if step == 0:
            forward(w_o, parts[0])
        attended = [o] + [x_shift(o, t) for t in (1, 2, 3)]
        sent = core_swap(project(send_place, attended, w_o))
        kept = project(keep_place, attended, w_o)
        own_sum, *sends = call(
            core_sum_kernel, [((TOK, 2 * W), F32)] + [((TOK, 2 * W), BF16)] * 3, n_in=2
        )(kept, sent)
        got = [y_shift(sends[s - 1], -s) for s in (1, 2, 3)]
        return call(y_sum_kernel, [((TOK, 2 * W), BF16)], n_in=7)(own_sum, *got, gate, keep, pair)[0]

    share = layer(pair, 0)
    first = (share.astype(F32) + head_swap(share, 2).astype(F32)).astype(BF16)
    second = pick(dest_block == 0, fresh_pair, first)
    share = layer(second, 1)
    mine_half = pick(zh == 0, share[:, :W], share[:, W:])
    other_half = pick(zh == 0, share[:, W:], share[:, :W])
    return (turned(mine_half, 0, 1).astype(F32) + turned(other_half, 1, 1).astype(F32)).astype(BF16)


def solution(mesh):
    return jax.shard_map(
        on_device,
        mesh=mesh,
        in_specs=(
            P("ctx", "head"),
            P(),
            P(None, "ctx", "head"),
            P("head", "ctx"),
            P(),
            P(),
            P(),
            P(),
        ),
        out_specs=P("ctx", "head"),
        check_vma=False,
    )
```
